128 devices in a mesh: lon: 32 (over y, x_hi, z), lat: 4 (over x_lo, core).
Axes of the slice: x: 4 (x_hi: 2, x_lo: 2; x = x_hi * 2 + x_lo), y: 4, z: 4, core: 2. Of those that a mesh axis runs over, the one named last changes fastest.
Arguments:
- field: bfloat16 [8, 96, 147456], P(None, 'lat', 'lon'), may hold values from -6 to 6
- cotangent: bfloat16 [8, 96, 147456], P(None, 'lat', 'lon'), may hold values from -6 to 6
- fine_gain_a: float32 [192], replicated, may hold values from 0.25 to 1.75
- fine_qkv: bfloat16 [192, 576], replicated, may hold values from -0.4375 to 0.4375
- fine_out: bfloat16 [192, 192], replicated, may hold values from -0.4375 to 0.4375
- fine_bias: bfloat16 [6, 16, 20736], P(None, 'lat'), may hold values from -6 to 6
- fine_gain_b: float32 [192], replicated, may hold values from 0.25 to 1.75
- fine_in: bfloat16 [192, 768], replicated, may hold values from -0.4375 to 0.4375
- fine_back: bfloat16 [192, 768], replicated, may hold values from -0.21875 to 0.21875
- merge_gain: float32 [768], replicated, may hold values from 0.25 to 1.75
- merge_weight: bfloat16 [768, 384], replicated, may hold values from -0.21875 to 0.21875
- coarse_gain_a: float32 [384], replicated, may hold values from 0.25 to 1.75
- coarse_qkv: bfloat16 [384, 1152], replicated, may hold values from -0.3125 to 0.3125
- coarse_out: bfloat16 [384, 384], replicated, may hold values from -0.3125 to 0.3125
- coarse_bias: bfloat16 [12, 8, 20736], P(None, 'lat'), may hold values from -6 to 6
- coarse_gain_b: float32 [384], replicated, may hold values from 0.25 to 1.75
- coarse_in: bfloat16 [384, 1536], replicated, may hold values from -0.3125 to 0.3125
- coarse_back: bfloat16 [384, 1536], replicated, may hold values from -0.15625 to 0.15625
- up_weight: bfloat16 [384, 768], replicated, may hold values from -0.3125 to 0.3125
Outputs:
- output: bfloat16 [8, 96, 147456], P(None, 'lat', 'lon')
- up_grad: float32 [384, 768], replicated
The draws below stay inside these ranges and needn't reach their ends.
All inputs are finite; a program needn't handle non-finite values.
Results may differ from the reference program's by a relative error of at most 0.02.
Values may be sent and summed in bfloat16 or wider, within the bound.
No kernel may reach another device: no remote copies, remote signals or barrier semaphores. Data moves between devices by JAX's collectives and lax.ppermute only.
A program may use at most 128 MiB of HBM per device.

```python
import jax
import jax.numpy as jnp
from jax import lax

HEADS = 6
LEV = 8
C = 192
NLAT = 96
NLON = 768


def block_scale(key, shape, split, low, high):
    level, own = 1.0, jax.random.fold_in(key, 6)
    for axis_at, blocks in split:
        steps = jnp.exp(jax.random.uniform(jax.random.fold_in(own, axis_at), (blocks,), jnp.float32, low / len(split), high / len(split)))
        level = level * jnp.repeat(steps, shape[axis_at] // blocks).reshape([-1 if axis == axis_at else 1 for axis in range(len(shape))])
    return level


def bell_draw(key, dims, scale, most, pieces=(), kind=jnp.bfloat16):
    drawn = jax.random.normal(key, dims, jnp.float32) * scale
    if len(pieces) > 0:
        drawn = block_scale(key, dims, pieces, -0.22, 0.18) * drawn
    return jnp.clip(drawn, min=-most, max=most).astype(kind)


def setup_inputs(seed: int = 0) -> dict:
    seeds = jax.random.split(jax.random.key(seed), 20)
    return {
        "field": bell_draw(seeds[0], (LEV, NLAT, NLON * C), 1.0, 6.0, ((1, 4), (2, 32))),
        "cotangent": bell_draw(seeds[1], (LEV, NLAT, NLON * C), 1.0, 6.0, ((1, 4), (2, 32))),
        "fine_gain_a": jnp.clip(1.0 + 0.15 * jax.random.normal(seeds[2], (C,), jnp.float32), 0.25, 1.75),
        "fine_qkv": bell_draw(seeds[3], (C, 3 * C), C ** -0.5, 0.4375),
        "fine_out": bell_draw(seeds[4], (C, C), C ** -0.5, 0.4375),
        "fine_bias": bell_draw(seeds[5], (HEADS, NLAT // 6, 144 * 144), 1.0, 6.0, ((1, 4),)),
        "fine_gain_b": jnp.clip(1.0 + 0.15 * jax.random.normal(seeds[6], (C,), jnp.float32), 0.25, 1.75),
        "fine_in": bell_draw(seeds[7], (C, 4 * C), C ** -0.5, 0.4375),
        "fine_back": bell_draw(seeds[8], (C, 4 * C), (4 * C) ** -0.5, 0.21875),
        "merge_gain": jnp.clip(1.0 + 0.15 * jax.random.normal(seeds[9], (4 * C,), jnp.float32), 0.25, 1.75),
        "merge_weight": bell_draw(seeds[10], (4 * C, 2 * C), (4 * C) ** -0.5, 0.21875),
        "coarse_gain_a": jnp.clip(1.0 + 0.15 * jax.random.normal(seeds[11], (2 * C,), jnp.float32), 0.25, 1.75),
        "coarse_qkv": bell_draw(seeds[12], (2 * C, 6 * C), (2 * C) ** -0.5, 0.3125),
        "coarse_out": bell_draw(seeds[13], (2 * C, 2 * C), (2 * C) ** -0.5, 0.3125),
        "coarse_bias": bell_draw(seeds[14], (2 * HEADS, NLAT // 12, 144 * 144), 1.0, 6.0, ((1, 4),)),
        "coarse_gain_b": jnp.clip(1.0 + 0.15 * jax.random.normal(seeds[15], (2 * C,), jnp.float32), 0.25, 1.75),
        "coarse_in": bell_draw(seeds[16], (2 * C, 8 * C), (2 * C) ** -0.5, 0.3125),
        "coarse_back": bell_draw(seeds[17], (2 * C, 8 * C), (8 * C) ** -0.5, 0.15625),
        "up_weight": bell_draw(seeds[18], (2 * C, 4 * C), (2 * C) ** -0.5, 0.3125),
    }


def layer_norm(value, gain):
    center = value - lax.optimization_barrier(jnp.mean(value, axis=-1, keepdims=True))
    spread = lax.optimization_barrier(jnp.mean(center * center, axis=-1, keepdims=True))
    return center * lax.rsqrt(spread + 1e-05) * gain

def window_block(field_in, gain_a, w_qkv, w_out, bias, gain_b, w_in, w_back):
    heads = bias.shape[0]
    levels, rows, cols, width = field_in.shape
    hdim = width // heads
    windows = field_in.reshape(levels // 2, 2, rows // 6, 6, cols // 12, 12, width)
    windows = windows.transpose(2, 0, 4, 1, 3, 5, 6).reshape(rows // 6, levels // 2 * (cols // 12), 144, width)
    tables = bias.reshape(heads, rows // 6, 144, 144).transpose(1, 0, 2, 3)

    def single(item):
        tokens, table = item
        count = tokens.shape[0]
        flat = tokens.reshape(count * 144, width).astype(jnp.float32)
        normed = layer_norm(flat, gain_a).astype(jnp.bfloat16)
        packed = jnp.dot(normed, w_qkv, preferred_element_type=jnp.float32).astype(jnp.bfloat16)
        packed = packed.reshape(count, 144, 3, heads, hdim).astype(jnp.float32)
        scores = jnp.einsum('nqhd,nkhd->nhqk', packed[:, :, 0], packed[:, :, 1]) * hdim ** (-0.5)
        scores = scores + table.astype(jnp.float32)[None]
        weights = jax.nn.softmax(scores, axis=-1).astype(jnp.bfloat16).astype(jnp.float32)
        mixed = jnp.einsum('nhqk,nkhd->nqhd', weights, packed[:, :, 2]).astype(jnp.bfloat16)
        mixed = mixed.reshape(count * 144, width)
        resid = flat + jnp.dot(mixed, w_out, preferred_element_type=jnp.float32)
        inner = layer_norm(resid, gain_b).astype(jnp.bfloat16)
        hidden = jax.nn.gelu(jnp.dot(inner, w_in, preferred_element_type=jnp.float32)).astype(jnp.bfloat16)
        result = resid + lax.dot_general(hidden, w_back, (((1,), (1,)), ((), ())), preferred_element_type=jnp.float32)
        return result.astype(jnp.bfloat16).reshape(count, 144, width)
    done = lax.map(single, (windows, tables))
    done = done.reshape(rows // 6, levels // 2, cols // 12, 2, 6, 12, width)
    return done.transpose(1, 3, 0, 4, 2, 5, 6).reshape(levels, rows, cols, width)

def group_patches(value):
    levels, rows, cols, width = value.shape
    grouped = value.reshape(levels, rows // 2, 2, cols // 2, 2, width).transpose(0, 1, 3, 2, 4, 5)
    return grouped.reshape(levels, rows // 2, cols // 2, 4 * width)

def reference(field, cotangent, fine_gain_a, fine_qkv, fine_out, fine_bias, fine_gain_b, fine_in, fine_back, merge_gain, merge_weight, coarse_gain_a, coarse_qkv, coarse_out, coarse_bias, coarse_gain_b, coarse_in, coarse_back, up_weight):
    width = fine_qkv.shape[0]
    levels, rows = (field.shape[0], field.shape[1])
    cols = field.shape[2] // width
    field = field.reshape(levels, rows, cols, width)
    cotangent = cotangent.reshape(levels, rows, cols, width)
    fine_done = window_block(jnp.roll(field, -6, axis=2), fine_gain_a, fine_qkv, fine_out, fine_bias, fine_gain_b, fine_in, fine_back)
    settled = jnp.roll(fine_done, 6, axis=2)
    normed = layer_norm(group_patches(settled).astype(jnp.float32), merge_gain).astype(jnp.bfloat16)
    coarse = jnp.dot(normed, merge_weight, preferred_element_type=jnp.float32).astype(jnp.bfloat16)
    coarse_mid = window_block(jnp.roll(coarse, -6, axis=2), coarse_gain_a, coarse_qkv, coarse_out, coarse_bias, coarse_gain_b, coarse_in, coarse_back)
    coarse_done = jnp.roll(coarse_mid, 6, axis=2)
    raised = jnp.dot(coarse_done, up_weight, preferred_element_type=jnp.float32)
    raised = raised.reshape(levels, rows // 2, cols // 2, 2, 2, width).transpose(0, 1, 3, 2, 4, 5)
    raised = raised.reshape(levels, rows, cols, width)
    output = (settled.astype(jnp.float32) + raised).astype(jnp.bfloat16)
    output = output.reshape(levels, rows, cols * width)
    flat_coarse = coarse_done.reshape(-1, 2 * width)
    flat_cot = group_patches(cotangent).reshape(-1, 4 * width)
    up_grad = lax.dot_general(flat_coarse, flat_cot, (((0,), (0,)), ((), ())), preferred_element_type=jnp.float32)
    return (output, up_grad)
```

```python
import functools
import jax
import jax.numpy as jnp
from jax import lax
from jax.experimental import pallas as pl
from jax.experimental.pallas import tpu as pltpu
from jax.sharding import PartitionSpec as P

BF = jnp.bfloat16
F32 = jnp.float32
NN = (((1,), (0,)), ((), ()))
NT = (((1,), (1,)), ((), ()))
TN = (((0,), (0,)), ((), ()))
LOG2E = 1.4426950408889634
HD = 32
UNITS = 2
LEAD = 0
MIB = 1024 * 1024


def mm(a, b, dims=NN):
    return lax.dot_general(a, b, dims, preferred_element_type=F32)


def row(ref):
    return ref[...].reshape(1, ref.shape[0])


def layer_norm(value, gain):
    center = value - jnp.mean(value, axis=-1, keepdims=True)
    spread = jnp.mean(center * center, axis=-1, keepdims=True)
    return center * lax.rsqrt(spread + 1e-05) * gain


def scaled_bias(bias_ref, table_ref, heads):
    for h in range(heads):
        for w in range(bias_ref.shape[1]):
            table_ref[w * heads + h] = bias_ref[h, w].astype(F32) * LOG2E


def put_rows(ref, at, value):
    for t in range(value.shape[1] // 128):
        ref[t, at : at + value.shape[0], :] = value[:, t * 128 : (t + 1) * 128]


def get_rows(ref, at, count):
    return jnp.concatenate([ref[t, at : at + count, :] for t in range(ref.shape[0])], axis=1)


def get_every_other(ref, at, count):
    return jnp.concatenate([ref[t, pl.ds(at, count, stride=2), :] for t in range(ref.shape[0])], axis=1)


def put_every_other(ref, at, value):
    for t in range(ref.shape[0]):
        ref[t, pl.ds(at, value.shape[0], stride=2), :] = value[:, t * 128 : (t + 1) * 128]


def tiled(value):
    short = -value.shape[1] % 128
    if short:
        value = jnp.concatenate([value, jnp.zeros((value.shape[0], short), value.dtype)], axis=1)
    return value


def window_block(result, v, ga, wq, wk, wv, w_out, table_ref, gb, w_in, w_back, mixed_ref):
    tokens, width = v.shape
    heads = width // HD
    aw = layer_norm(v, ga).astype(BF)
    yield
    q_all = (mm(aw, wq) * (LOG2E * HD**-0.5)).astype(BF)
    k_all = mm(aw, wk).astype(BF)
    v_all = mm(aw, wv).astype(BF)
    yield
    lane = lax.broadcasted_iota(jnp.int32, (144, 128), 1)
    ones = jnp.ones((144, 128), BF)
    for w in range(tokens // 144):
        rows = slice(w * 144, (w + 1) * 144)
        for t in range(-(-width // 128)):
            lanes = slice(t * 128, t * 128 + 128)
            total = jnp.zeros((144, 128), F32)
            count = jnp.ones((144, 128), F32)
            q, k = q_all[rows, lanes], k_all[rows, lanes]
            values = jnp.concatenate([v_all[rows, lanes], ones], axis=1)
            for j in range(min(4, heads - 4 * t)):
                mine = (lane >= j * HD) & (lane < j * HD + HD)
                s = mm(jnp.where(mine, q, jnp.zeros_like(q)), k, NT) + table_ref[w * heads + 4 * t + j]
                p = jnp.exp2(s - jnp.max(s, axis=1, keepdims=True)).astype(BF)
                o = mm(p, values)
                total = jnp.where(mine, o[:, :128], total)
                count = jnp.where(mine, o[:, 128:], count)
            mixed_ref[rows, lanes] = (total / count).astype(BF)
            yield
    r = v + mm(mixed_ref[:, :width], w_out)
    m = layer_norm(r, gb).astype(BF)
    yield
    u = jax.nn.gelu(mm(m, w_in)).astype(BF)
    yield
    result.append((r + mm(u, w_back, NT)).astype(BF))
    yield


def interleave(streams, lead):
    waiting = list(streams)
    for _ in range(lead):
        next(waiting[0], None)
    while waiting:
        waiting = [g for g in waiting if next(g, g) is not g]


def fine_moves():
    for l in range(2):
        for row in range(24):
            for c in range(2):
                yield l * 288 + c * 144 + row, (row // 6) * 144 + l * 72 + (row % 6) * 12 + c


def fine_kernel(
    left_ref, right_ref, bias_ref, ga_ref, wqkv_ref, wo_ref, gb_ref,
    wi_ref, wb_ref, mg_ref, mw_ref,
    out_left, out_right, coarse_left, coarse_right, nat_ref, win_ref, table_ref, mixed_ref, proj_ref,
):
    heads = bias_ref.shape[0]

    @pl.when(pl.program_id(0) == 0)
    def _():
        scaled_bias(bias_ref, table_ref, heads)
        width = wo_ref.shape[0]
        proj_ref[...] = jnp.zeros_like(proj_ref)
        for i in range(3):
            proj_ref[i, :, :width] = wqkv_ref[:, i * width : (i + 1) * width]

    units = left_ref.shape[0] // 2
    interleave(
        [
            fine_unit(
                u, (left_ref, right_ref), ga_ref, proj_ref, wo_ref, gb_ref, wi_ref, wb_ref, mg_ref, mw_ref,
                (out_left, out_right), coarse_left, coarse_right, nat_ref.at[u], win_ref.at[u], table_ref, mixed_ref.at[u],
            )
            for u in range(units)
        ],
        LEAD if units > 1 else 0,
    )


def fine_unit(
    u, halves, ga_ref, proj_ref, wo_ref, gb_ref, wi_ref, wb_ref, mg_ref, mw_ref,
    outs, coarse_left, coarse_right, nat_ref, win_ref, table_ref, mixed_ref,
):
    width = wo_ref.shape[0]
    pair = 2 * width
    for l in range(2):
        for s in range(2):
            for p in range(3):
                at = l * 288 + (s * 3 + p) * 24
                x = halves[s][2 * u + l, :, p * pair : (p + 1) * pair].astype(F32)
                put_rows(nat_ref, at, x[:, :256])
                put_rows(nat_ref, at + 144, pltpu.roll(x[:, 128:], 192, axis=1))
    for src, dst in fine_moves():
        for t in range(2):
            win_ref[t, pl.ds(dst, 6, stride=2), :] = nat_ref[t, pl.ds(src, 6, stride=24), :]
    v = get_rows(win_ref, 0, 576)[:, :width]
    yield
    result = []
    yield from window_block(
        result, v, row(ga_ref), proj_ref[0], proj_ref[1], proj_ref[2], wo_ref[...],
        table_ref, row(gb_ref), wi_ref[...], wb_ref[...], mixed_ref,
    )
    done = result[0].astype(F32)
    put_rows(win_ref, 0, tiled(done))
    for src, dst in fine_moves():
        for t in range(2):
            nat_ref[t, pl.ds(src, 6, stride=24), :] = win_ref[t, pl.ds(dst, 6, stride=2), :]
    yield
    quarter = []
    for r in range(2):
        for c in range(2):
            quarter.append(
                jnp.concatenate(
                    [get_every_other(nat_ref, l * 288 + c * 144 + r, 72)[:, :width] for l in range(2)], axis=0
                )
            )
    mean = sum(jnp.sum(x, axis=-1, keepdims=True) for x in quarter) * (1.0 / (4 * width))
    center = [x - mean for x in quarter]
    spread = sum(jnp.sum(x * x, axis=-1, keepdims=True) for x in center) * (1.0 / (4 * width))
    scale = lax.rsqrt(spread + 1e-05)
    gains = row(mg_ref)
    coarse = 0.0
    for i in range(4):
        n = (center[i] * scale * gains[:, i * width : (i + 1) * width]).astype(BF)
        coarse = coarse + mm(n, mw_ref[i * width : (i + 1) * width])
    for l in range(2):
        coarse_left[u, l] = coarse[l * 72 : l * 72 + 36].astype(BF)
        coarse_right[u, l] = coarse[l * 72 + 36 : l * 72 + 72].astype(BF)
    yield
    low = lax.broadcasted_iota(jnp.int32, (24, 128), 1) < 64
    for l in range(2):
        for s in range(2):
            for p in range(3):
                at = l * 288 + (s * 3 + p) * 24
                even = get_rows(nat_ref, at, 24)
                odd = pltpu.roll(get_rows(nat_ref, at + 144, 24), 64, axis=1)
                middle = jnp.where(low, even[:, 128:], odd[:, :128])
                outs[s][2 * u + l, :, p * pair : (p + 1) * pair] = jnp.concatenate(
                    [even[:, :128], middle, odd[:, 128:]], axis=1
                ).astype(BF)


def coarse_kernel(
    g0, g1, g2, g3, cot_ref, cot_next_ref, bias_ref, ga_ref, wqkv_ref, wo_ref, gb_ref,
    wi_ref, wb_ref,
    done_own, done_first, done_last, packed_ref, nat_ref, win_ref, table_ref, mixed_ref, grad_ref,
):
    heads = bias_ref.shape[0]

    @pl.when(pl.program_id(0) == 0)
    def _():
        scaled_bias(bias_ref, table_ref, heads)
        grad_ref[...] = jnp.zeros_like(grad_ref)

    units = g0.shape[0]
    interleave(
        [
            coarse_unit(
                u, (g0, g1, g2, g3), cot_ref, cot_next_ref, ga_ref, wqkv_ref, wo_ref, gb_ref, wi_ref, wb_ref,
                done_own, done_last, grad_ref, nat_ref.at[u], win_ref.at[u], table_ref, mixed_ref.at[u],
            )
            for u in range(units)
        ],
        LEAD if units > 1 else 0,
    )

    @pl.when(pl.program_id(0) == 0)
    def _():
        done_first[...] = done_last[...]

    @pl.when(pl.program_id(0) == pl.num_programs(0) - 1)
    def _():
        for j in range(128):
            t, b = divmod(j, 24)
            packed_ref[j, :16, :] = grad_ref[b * 16 : b * 16 + 16, t * 128 : (t + 1) * 128].astype(BF)
            packed_ref[j, 16:, :] = grad_ref[128 + 2 * j : 130 + 2 * j, 640:].astype(BF)


def sum_kernel(in_ref, out_ref):
    total = in_ref[0].astype(F32)
    for j in range(1, 128):
        total = total + in_ref[j].astype(F32)
    total = total.astype(BF)
    for j in range(128):
        out_ref[j] = total


def unpack_kernel(in_ref, out_ref):
    for j in range(128):
        t, b = divmod(j, 24)
        out_ref[b * 16 : b * 16 + 16, t * 128 : (t + 1) * 128] = in_ref[j, :16, :].astype(F32)
        out_ref[128 + 2 * j : 130 + 2 * j, 640:] = in_ref[j, 16:, :].astype(F32)


def coarse_unit(
    u, groups, cot_ref, cot_next_ref, ga_ref, wqkv_ref, wo_ref, gb_ref, wi_ref, wb_ref,
    done_own, done_next, grad_ref, nat_ref, win_ref, table_ref, mixed_ref,
):
    width = wo_ref.shape[0]
    for l in range(2):
        for i, g in enumerate(groups):
            put_rows(nat_ref, l * 144 + i * 36, g[u, l].astype(F32))
    moves = [(l * 144 + row, (row // 6) * 144 + l * 72 + (row % 6) * 12) for l in range(2) for row in range(12)]
    for src, dst in moves:
        for t in range(3):
            win_ref[t, dst : dst + 12, :] = nat_ref[t, pl.ds(src, 12, stride=12), :]
    yield
    result = []
    yield from window_block(
        result, get_rows(win_ref, 0, 288), row(ga_ref), wqkv_ref[:, :width], wqkv_ref[:, width : 2 * width],
        wqkv_ref[:, 2 * width :], wo_ref[...],
        table_ref, row(gb_ref), wi_ref[...], wb_ref[...], mixed_ref,
    )
    done = result[0]
    put_rows(win_ref, 0, done.astype(F32))
    for src, dst in moves:
        for t in range(3):
            nat_ref[t, pl.ds(src, 12, stride=12), :] = win_ref[t, dst : dst + 12, :]
    yield
    for half, ref, out in ((0, cot_ref, done_own), (1, cot_next_ref, done_next)):
        tokens = jnp.concatenate([get_rows(nat_ref, l * 144 + half * 72, 72) for l in range(2)], axis=0).astype(BF)
        out[u] = tokens
        for l in range(2):
            for c in range(6):
                put_rows(win_ref, (l * 6 + c) * 24, ref[2 * u + l, :, c * width : (c + 1) * width].astype(F32))
        for r in range(2):
            x = get_every_other(win_ref, r, 144).astype(BF)
            grad_ref[:, r * width : (r + 1) * width] += mm(tokens, x, TN)
        yield


def final_kernel(done_west, done_east, set0, set1, set2, set3, up_ref, *rest):
    out_ref, rows_ref = rest[-2:]
    width = done_west.shape[2]
    halves = (set0, set1, set2, set3)
    for e, done_ref in enumerate((done_west, done_east)):
        raised = mm(done_ref[0], up_ref[...])
        for r in range(2):
            put_every_other(rows_ref, r, raised[:, r * width : (r + 1) * width])
        for l in range(2):
            for c in range(6):
                base = halves[2 * e + c // 3][l, :, (c % 3) * width : (c % 3 + 1) * width]
                total = base.astype(F32) + get_rows(rows_ref, (l * 6 + c) * 24, 24)
                out_ref[l, :, (e * 6 + c) * width : (e * 6 + c + 1) * width] = total.astype(BF)


def whole(a):
    return pl.BlockSpec(a.shape, lambda i: (0,) * a.ndim)


def params(mib):
    return pltpu.CompilerParams(vmem_limit_bytes=mib * MIB, dimension_semantics=("arbitrary",))


def fine_call(left, left_at, right, right_at, consts):
    levels, rows, _ = left.shape
    half = 1152
    steps = levels // (2 * UNITS)

    def spec(at):
        return pl.BlockSpec((2 * UNITS, rows, half), lambda i: (i, 0, at))

    cspec = pl.BlockSpec((UNITS, 2, 36, 384), lambda i: (i, 0, 0, 0))
    return pl.pallas_call(
        fine_kernel,
        grid=(steps,),
        in_specs=[spec(left_at), spec(right_at)] + [whole(c) for c in consts],
        out_specs=[spec(0), spec(0), cspec, cspec],
        out_shape=[jax.ShapeDtypeStruct((levels, rows, half), BF)] * 2
        + [jax.ShapeDtypeStruct((steps * UNITS, 2, 36, 384), BF)] * 2,
        scratch_shapes=[
            pltpu.VMEM((UNITS, 2, 576, 128), F32),
            pltpu.VMEM((UNITS, 2, 576, 128), F32),
            pltpu.VMEM((24, 144, 144), F32),
            pltpu.VMEM((UNITS, 576, 256), BF),
            pltpu.VMEM((3, 192, 256), BF),
        ],
        compiler_params=params(56),
        cost_estimate=pl.CostEstimate(flops=3 * 10**9, bytes_accessed=6 * 10**6, transcendentals=10**6),
    )(left, right, *consts)


def coarse_call(groups, cot, cot_next, consts):
    steps = groups[0].shape[0] // UNITS
    gspec = pl.BlockSpec((UNITS, 2, 36, 384), lambda i: (i, 0, 0, 0))
    dspec = pl.BlockSpec((UNITS, 144, 384), lambda i: (i, 0, 0))
    return pl.pallas_call(
        coarse_kernel,
        grid=(steps,),
        in_specs=[gspec] * 4
        + [pl.BlockSpec((2 * UNITS, 24, 2304), lambda i: (i, 0, 1)), pl.BlockSpec((2 * UNITS, 24, 2304), lambda i: (i, 0, 0))]
        + [whole(c) for c in consts],
        out_specs=[dspec] + [pl.BlockSpec((UNITS, 144, 384), lambda i: (0, 0, 0))] * 2
        + [pl.BlockSpec((128, 18, 128), lambda i: (0, 0, 0))],
        out_shape=[jax.ShapeDtypeStruct((steps * UNITS, 144, 384), BF)]
        + [jax.ShapeDtypeStruct((UNITS, 144, 384), BF)] * 2
        + [jax.ShapeDtypeStruct((128, 18, 128), BF)],
        scratch_shapes=[
            pltpu.VMEM((UNITS, 3, 288, 128), F32),
            pltpu.VMEM((UNITS, 3, 288, 128), F32),
            pltpu.VMEM((24, 144, 144), F32),
            pltpu.VMEM((UNITS, 288, 384), BF),
            pltpu.VMEM((384, 768), F32),
        ],
        compiler_params=params(56),
        cost_estimate=pl.CostEstimate(flops=5 * 10**9, bytes_accessed=8 * 10**6, transcendentals=10**6),
    )(*groups, cot, cot_next, *consts)


def final_call(first, done_west, done_east, quarters, up, below=None):
    steps = done_west.shape[0]
    sspec = pl.BlockSpec((2, 24, 1152), lambda i: (i + first, 0, 0))
    extra = () if below is None else (below,)
    return pl.pallas_call(
        final_kernel,
        grid=(steps,),
        in_specs=[
            pl.BlockSpec((1, 144, 384), lambda i: (i, 0, 0)),
            pl.BlockSpec((1, 144, 384), lambda i: (i + first, 0, 0)),
        ]
        + [sspec] * 4
        + [whole(up)]
        + [pl.BlockSpec(memory_space=pl.ANY)] * len(extra),
        out_specs=pl.BlockSpec((2, 24, 4608), lambda i: (i + first, 0, 0)),
        out_shape=jax.ShapeDtypeStruct((8, 24, 4608), BF),
        scratch_shapes=[pltpu.VMEM((3, 288, 128), F32)],
        input_output_aliases={7: 0} if extra else {},
        compiler_params=params(32),
        cost_estimate=pl.CostEstimate(flops=8 * 10**8, bytes_accessed=6 * 10**6, transcendentals=0),
    )(done_west, done_east, *quarters, up, *extra)


def passed_along(block, axis, distance):
    n = lax.axis_size(axis)
    return lax.ppermute(block, axis, [((i - distance) % n, i) for i in range(n)])


def packed_call(kernel, packed, shape, dtype):
    return pl.pallas_call(
        kernel,
        out_shape=jax.ShapeDtypeStruct(shape, dtype),
        in_specs=[pl.BlockSpec(memory_space=pltpu.VMEM)],
        out_specs=pl.BlockSpec(memory_space=pltpu.VMEM),
        compiler_params=pltpu.CompilerParams(vmem_limit_bytes=16 * MIB),
    )(packed)


def reduce_everywhere(packed, meanwhile):
    axes = ("lon", "lat")
    if lax.axis_size("lon") * lax.axis_size("lat") != packed.shape[0]:
        packed = lax.psum(packed.astype(F32), axes).astype(BF)
    else:
        parts = lax.all_to_all(packed, axes, 0, 0)
        parts, meanwhile = lax.optimization_barrier((parts, meanwhile))
        packed = lax.all_to_all(packed_call(sum_kernel, parts, packed.shape, BF), axes, 0, 0)
    return packed_call(unpack_kernel, packed, (384, 768), F32), meanwhile


def shards(
    field, cotangent,
    fine_gain_a, fine_qkv, fine_out, fine_bias, fine_gain_b, fine_in, fine_back,
    merge_gain, merge_weight,
    coarse_gain_a, coarse_qkv, coarse_out, coarse_bias, coarse_gain_b, coarse_in, coarse_back,
    up_weight,
):
    width = fine_qkv.shape[0]
    half = 6 * width
    halo = passed_along(field[:, :, :half], "lon", -1)
    cot_next = passed_along(cotangent[:, :, : 2 * half], "lon", -1)
    fine_consts = (
        fine_bias.reshape(fine_bias.shape[0], fine_bias.shape[1], 144, 144),
        fine_gain_a, fine_qkv, fine_out, fine_gain_b, fine_in, fine_back, merge_gain, merge_weight,
    )
    coarse_consts = (
        coarse_bias.reshape(coarse_bias.shape[0], coarse_bias.shape[1], 144, 144),
        coarse_gain_a, coarse_qkv, coarse_out, coarse_gain_b, coarse_in, coarse_back,
    )
    a_left, a_right, ca_left, ca_right = fine_call(field, 1, field, 2, fine_consts)
    ca_next = passed_along(ca_left, "lon", -1)
    b_left, b_right, cb_left, cb_right = fine_call(field, 3, halo, 0, fine_consts)
    b_prev = passed_along(b_right, "lon", 1)
    done_own, done_first, done_last, packed = coarse_call(
        (ca_right, cb_left, cb_right, ca_next), cotangent, cot_next, coarse_consts
    )
    first_prev = passed_along(done_first, "lon", 1)
    last_prev = passed_along(done_last, "lon", 1)
    packed, b_prev = lax.optimization_barrier((packed, b_prev))
    up_grad, first_prev = reduce_everywhere(packed, first_prev)
    quarters = (b_prev, a_left, a_right, b_left)
    output = final_call(0, first_prev, done_own, quarters, up_weight)
    output = final_call(done_first.shape[0], last_prev, done_own, quarters, up_weight, output)
    return output, up_grad


def solution(mesh):
    lat = P(None, "lat", None)
    split = P(None, "lat", "lon")
    return jax.shard_map(
        shards,
        mesh=mesh,
        in_specs=(split, split, P(), P(), P(), lat) + (P(),) * 8 + (lat,) + (P(),) * 4,
        out_specs=(split, P()),
        check_vma=False,
    )
```

```python
import functools
import jax
import jax.numpy as jnp
from jax import lax
from jax.experimental import pallas as pl
from jax.experimental.pallas import tpu as pltpu
from jax.sharding import PartitionSpec as P

BF = jnp.bfloat16
F32 = jnp.float32
NN = (((1,), (0,)), ((), ()))
NT = (((1,), (1,)), ((), ()))
TN = (((0,), (0,)), ((), ()))
LOG2E = 1.4426950408889634
HD = 32
UNITS = 2
LEAD = 0
MIB = 1024 * 1024


def mm(a, b, dims=NN):
    return lax.dot_general(a, b, dims, preferred_element_type=F32)


def row(ref):
    return ref[...].reshape(1, ref.shape[0])


def layer_norm(value, gain):
    center = value - jnp.mean(value, axis=-1, keepdims=True)
    spread = jnp.mean(center * center, axis=-1, keepdims=True)
    return center * lax.rsqrt(spread + 1e-05) * gain


def scaled_bias(bias_ref, table_ref, heads):
    for h in range(heads):
        for w in range(bias_ref.shape[1]):
            table_ref[w * heads + h] = bias_ref[h, w].astype(F32) * LOG2E


def put_rows(ref, at, value):
    for t in range(value.shape[1] // 128):
        ref[t, at : at + value.shape[0], :] = value[:, t * 128 : (t + 1) * 128]


def get_rows(ref, at, count):
    return jnp.concatenate([ref[t, at : at + count, :] for t in range(ref.shape[0])], axis=1)


def get_every_other(ref, at, count):
    return jnp.concatenate([ref[t, pl.ds(at, count, stride=2), :] for t in range(ref.shape[0])], axis=1)


def put_every_other(ref, at, value):
    for t in range(ref.shape[0]):
        ref[t, pl.ds(at, value.shape[0], stride=2), :] = value[:, t * 128 : (t + 1) * 128]


def tiled(value):
    short = -value.shape[1] % 128
    if short:
        value = jnp.concatenate([value, jnp.zeros((value.shape[0], short), value.dtype)], axis=1)
    return value


def window_block(result, v, ga, wq, wk, wv, w_out, table_ref, gb, w_in, w_back, mixed_ref):
    tokens, width = v.shape
    heads = width // HD
    aw = layer_norm(v, ga).astype(BF)
    yield
    q_all = (mm(aw, wq) * (LOG2E * HD**-0.5)).astype(BF)
    k_all = mm(aw, wk).astype(BF)
    v_all = mm(aw, wv).astype(BF)
    yield
    lane = lax.broadcasted_iota(jnp.int32, (144, 128), 1)
    ones = jnp.ones((144, 128), BF)
    for w in range(tokens // 144):
        rows = slice(w * 144, (w + 1) * 144)
        for t in range(-(-width // 128)):
            lanes = slice(t * 128, t * 128 + 128)
            total = jnp.zeros((144, 128), F32)
            count = jnp.ones((144, 128), F32)
            q, k = q_all[rows, lanes], k_all[rows, lanes]
            values = jnp.concatenate([v_all[rows, lanes], ones], axis=1)
            for j in range(min(4, heads - 4 * t)):
                mine = (lane >= j * HD) & (lane < j * HD + HD)
                s = mm(jnp.where(mine, q, jnp.zeros_like(q)), k, NT) + table_ref[w * heads + 4 * t + j]
                p = jnp.exp2(s - jnp.max(s, axis=1, keepdims=True)).astype(BF)
                o = mm(p, values)
                total = jnp.where(mine, o[:, :128], total)
                count = jnp.where(mine, o[:, 128:], count)
            mixed_ref[rows, lanes] = (total / count).astype(BF)
            yield
    r = v + mm(mixed_ref[:, :width], w_out)
    m = layer_norm(r, gb).astype(BF)
    yield
    u = jax.nn.gelu(mm(m, w_in)).astype(BF)
    yield
    result.append((r + mm(u, w_back, NT)).astype(BF))
    yield


def interleave(streams, lead):
    waiting = list(streams)
    for _ in range(lead):
        next(waiting[0], None)
    while waiting:
        waiting = [g for g in waiting if next(g, g) is not g]


def fine_moves():
    for l in range(2):
        for row in range(24):
            for c in range(2):
                yield l * 288 + c * 144 + row, (row // 6) * 144 + l * 72 + (row % 6) * 12 + c


def fine_kernel(
    left_ref, right_ref, bias_ref, ga_ref, wqkv_ref, wo_ref, gb_ref,
    wi_ref, wb_ref, mg_ref, mw_ref,
    out_left, out_right, coarse_left, coarse_right, nat_ref, win_ref, table_ref, mixed_ref, proj_ref,
):
    heads = bias_ref.shape[0]

    @pl.when(pl.program_id(0) == 0)
    def _():
        scaled_bias(bias_ref, table_ref, heads)
        width = wo_ref.shape[0]
        proj_ref[...] = jnp.zeros_like(proj_ref)
        for i in range(3):
            proj_ref[i, :, :width] = wqkv_ref[:, i * width : (i + 1) * width]

    units = left_ref.shape[0] // 2
    interleave(
        [
            fine_unit(
                u, (left_ref, right_ref), ga_ref, proj_ref, wo_ref, gb_ref, wi_ref, wb_ref, mg_ref, mw_ref,
                (out_left, out_right), coarse_left, coarse_right, nat_ref.at[u], win_ref.at[u], table_ref, mixed_ref.at[u],
            )
            for u in range(units)
        ],
        LEAD if units > 1 else 0,
    )


def fine_unit(
    u, halves, ga_ref, proj_ref, wo_ref, gb_ref, wi_ref, wb_ref, mg_ref, mw_ref,
    outs, coarse_left, coarse_right, nat_ref, win_ref, table_ref, mixed_ref,
):
    width = wo_ref.shape[0]
    pair = 2 * width
    for l in range(2):
        for s in range(2):
            for p in range(3):
                at = l * 288 + (s * 3 + p) * 24
                x = halves[s][2 * u + l, :, p * pair : (p + 1) * pair].astype(F32)
                put_rows(nat_ref, at, x[:, :256])
                put_rows(nat_ref, at + 144, pltpu.roll(x[:, 128:], 192, axis=1))
    for src, dst in fine_moves():
        for t in range(2):
            win_ref[t, pl.ds(dst, 6, stride=2), :] = nat_ref[t, pl.ds(src, 6, stride=24), :]
    v = get_rows(win_ref, 0, 576)[:, :width]
    yield
    result = []
    yield from window_block(
        result, v, row(ga_ref), proj_ref[0], proj_ref[1], proj_ref[2], wo_ref[...],
        table_ref, row(gb_ref), wi_ref[...], wb_ref[...], mixed_ref,
    )
    done = result[0].astype(F32)
    put_rows(win_ref, 0, tiled(done))
    for src, dst in fine_moves():
        for t in range(2):
            nat_ref[t, pl.ds(src, 6, stride=24), :] = win_ref[t, pl.ds(dst, 6, stride=2), :]
    yield
    quarter = []
    for r in range(2):
        for c in range(2):
            quarter.append(
                jnp.concatenate(
                    [get_every_other(nat_ref, l * 288 + c * 144 + r, 72)[:, :width] for l in range(2)], axis=0
                )
            )
    mean = sum(jnp.sum(x, axis=-1, keepdims=True) for x in quarter) * (1.0 / (4 * width))
    center = [x - mean for x in quarter]
    spread = sum(jnp.sum(x * x, axis=-1, keepdims=True) for x in center) * (1.0 / (4 * width))
    scale = lax.rsqrt(spread + 1e-05)
    gains = row(mg_ref)
    coarse = 0.0
    for i in range(4):
        n = (center[i] * scale * gains[:, i * width : (i + 1) * width]).astype(BF)
        coarse = coarse + mm(n, mw_ref[i * width : (i + 1) * width])
    for l in range(2):
        coarse_left[u, l] = coarse[l * 72 : l * 72 + 36].astype(BF)
        coarse_right[u, l] = coarse[l * 72 + 36 : l * 72 + 72].astype(BF)
    yield
    low = lax.broadcasted_iota(jnp.int32, (24, 128), 1) < 64
    for l in range(2):
        for s in range(2):
            for p in range(3):
                at = l * 288 + (s * 3 + p) * 24
                even = get_rows(nat_ref, at, 24)
                odd = pltpu.roll(get_rows(nat_ref, at + 144, 24), 64, axis=1)
                middle = jnp.where(low, even[:, 128:], odd[:, :128])
                outs[s][2 * u + l, :, p * pair : (p + 1) * pair] = jnp.concatenate(
                    [even[:, :128], middle, odd[:, 128:]], axis=1
                ).astype(BF)


def coarse_kernel(
    g0, g1, g2, g3, cot_ref, cot_next_ref, bias_ref, ga_ref, wqkv_ref, wo_ref, gb_ref,
    wi_ref, wb_ref,
    done_own, done_next, packed_ref, nat_ref, win_ref, table_ref, mixed_ref, grad_ref,
):
    heads = bias_ref.shape[0]

    @pl.when(pl.program_id(0) == 0)
    def _():
        scaled_bias(bias_ref, table_ref, heads)
        grad_ref[...] = jnp.zeros_like(grad_ref)

    units = g0.shape[0]
    interleave(
        [
            coarse_unit(
                u, (g0, g1, g2, g3), cot_ref, cot_next_ref, ga_ref, wqkv_ref, wo_ref, gb_ref, wi_ref, wb_ref,
                done_own, done_next, grad_ref, nat_ref.at[u], win_ref.at[u], table_ref, mixed_ref.at[u],
            )
            for u in range(units)
        ],
        LEAD if units > 1 else 0,
    )

    @pl.when(pl.program_id(0) == pl.num_programs(0) - 1)
    def _():
        for j in range(128):
            t, b = divmod(j, 24)
            packed_ref[j, :16, :] = grad_ref[b * 16 : b * 16 + 16, t * 128 : (t + 1) * 128].astype(BF)
            packed_ref[j, 16:, :] = grad_ref[128 + 2 * j : 130 + 2 * j, 640:].astype(BF)


def sum_kernel(in_ref, out_ref):
    total = in_ref[0].astype(F32)
    for j in range(1, 128):
        total = total + in_ref[j].astype(F32)
    total = total.astype(BF)
    for j in range(128):
        out_ref[j] = total


def unpack_kernel(in_ref, out_ref):
    for j in range(128):
        t, b = divmod(j, 24)
        out_ref[b * 16 : b * 16 + 16, t * 128 : (t + 1) * 128] = in_ref[j, :16, :].astype(F32)
        out_ref[128 + 2 * j : 130 + 2 * j, 640:] = in_ref[j, 16:, :].astype(F32)


def coarse_unit(
    u, groups, cot_ref, cot_next_ref, ga_ref, wqkv_ref, wo_ref, gb_ref, wi_ref, wb_ref,
    done_own, done_next, grad_ref, nat_ref, win_ref, table_ref, mixed_ref,
):
    width = wo_ref.shape[0]
    for l in range(2):
        for i, g in enumerate(groups):
            put_rows(nat_ref, l * 144 + i * 36, g[u, l].astype(F32))
    moves = [(l * 144 + row, (row // 6) * 144 + l * 72 + (row % 6) * 12) for l in range(2) for row in range(12)]
    for src, dst in moves:
        for t in range(3):
            win_ref[t, dst : dst + 12, :] = nat_ref[t, pl.ds(src, 12, stride=12), :]
    yield
    result = []
    yield from window_block(
        result, get_rows(win_ref, 0, 288), row(ga_ref), wqkv_ref[:, :width], wqkv_ref[:, width : 2 * width],
        wqkv_ref[:, 2 * width :], wo_ref[...],
        table_ref, row(gb_ref), wi_ref[...], wb_ref[...], mixed_ref,
    )
    done = result[0]
    put_rows(win_ref, 0, done.astype(F32))
    for src, dst in moves:
        for t in range(3):
            nat_ref[t, pl.ds(src, 12, stride=12), :] = win_ref[t, dst : dst + 12, :]
    yield
    for half, ref, out in ((0, cot_ref, done_own), (1, cot_next_ref, done_next)):
        tokens = jnp.concatenate([get_rows(nat_ref, l * 144 + half * 72, 72) for l in range(2)], axis=0).astype(BF)
        out[u] = tokens
        for l in range(2):
            for c in range(6):
                put_rows(win_ref, (l * 6 + c) * 24, ref[2 * u + l, :, c * width : (c + 1) * width].astype(F32))
        for r in range(2):
            x = get_every_other(win_ref, r, 144).astype(BF)
            grad_ref[:, r * width : (r + 1) * width] += mm(tokens, x, TN)
        yield


def final_kernel(done_west, done_east, set0, set1, set2, set3, up_ref, out_ref, rows_ref):
    width = done_west.shape[2]
    halves = (set0, set1, set2, set3)
    for e, done_ref in enumerate((done_west, done_east)):
        raised = mm(done_ref[0], up_ref[...])
        for r in range(2):
            put_every_other(rows_ref, r, raised[:, r * width : (r + 1) * width])
        for l in range(2):
            for c in range(6):
                base = halves[2 * e + c // 3][l, :, (c % 3) * width : (c % 3 + 1) * width]
                total = base.astype(F32) + get_rows(rows_ref, (l * 6 + c) * 24, 24)
                out_ref[l, :, (e * 6 + c) * width : (e * 6 + c + 1) * width] = total.astype(BF)


def whole(a):
    return pl.BlockSpec(a.shape, lambda i: (0,) * a.ndim)


def params(mib):
    return pltpu.CompilerParams(vmem_limit_bytes=mib * MIB, dimension_semantics=("arbitrary",))


def fine_call(left, left_at, right, right_at, consts):
    levels, rows, _ = left.shape
    half = 1152
    steps = levels // (2 * UNITS)

    def spec(at):
        return pl.BlockSpec((2 * UNITS, rows, half), lambda i: (i, 0, at))

    cspec = pl.BlockSpec((UNITS, 2, 36, 384), lambda i: (i, 0, 0, 0))
    return pl.pallas_call(
        fine_kernel,
        grid=(steps,),
        in_specs=[spec(left_at), spec(right_at)] + [whole(c) for c in consts],
        out_specs=[spec(0), spec(0), cspec, cspec],
        out_shape=[jax.ShapeDtypeStruct((levels, rows, half), BF)] * 2
        + [jax.ShapeDtypeStruct((steps * UNITS, 2, 36, 384), BF)] * 2,
        scratch_shapes=[
            pltpu.VMEM((UNITS, 2, 576, 128), F32),
            pltpu.VMEM((UNITS, 2, 576, 128), F32),
            pltpu.VMEM((24, 144, 144), F32),
            pltpu.VMEM((UNITS, 576, 256), BF),
            pltpu.VMEM((3, 192, 256), BF),
        ],
        compiler_params=params(56),
        cost_estimate=pl.CostEstimate(flops=3 * 10**9, bytes_accessed=6 * 10**6, transcendentals=10**6),
    )(left, right, *consts)


def coarse_call(groups, cot, cot_next, consts):
    steps = groups[0].shape[0] // UNITS
    gspec = pl.BlockSpec((UNITS, 2, 36, 384), lambda i: (i, 0, 0, 0))
    dspec = pl.BlockSpec((UNITS, 144, 384), lambda i: (i, 0, 0))
    return pl.pallas_call(
        coarse_kernel,
        grid=(steps,),
        in_specs=[gspec] * 4
        + [pl.BlockSpec((2 * UNITS, 24, 2304), lambda i: (i, 0, 1)), pl.BlockSpec((2 * UNITS, 24, 2304), lambda i: (i, 0, 0))]
        + [whole(c) for c in consts],
        out_specs=[dspec, dspec, pl.BlockSpec((128, 18, 128), lambda i: (0, 0, 0))],
        out_shape=[jax.ShapeDtypeStruct((steps * UNITS, 144, 384), BF)] * 2
        + [jax.ShapeDtypeStruct((128, 18, 128), BF)],
        scratch_shapes=[
            pltpu.VMEM((UNITS, 3, 288, 128), F32),
            pltpu.VMEM((UNITS, 3, 288, 128), F32),
            pltpu.VMEM((24, 144, 144), F32),
            pltpu.VMEM((UNITS, 288, 384), BF),
            pltpu.VMEM((384, 768), F32),
        ],
        compiler_params=params(56),
        cost_estimate=pl.CostEstimate(flops=5 * 10**9, bytes_accessed=8 * 10**6, transcendentals=10**6),
    )(*groups, cot, cot_next, *consts)


def final_call(done_west, done_east, quarters, up):
    steps = done_west.shape[0]
    dspec = pl.BlockSpec((1, 144, 384), lambda i: (i, 0, 0))
    sspec = pl.BlockSpec((2, 24, 1152), lambda i: (i, 0, 0))
    return pl.pallas_call(
        final_kernel,
        grid=(steps,),
        in_specs=[dspec] * 2 + [sspec] * 4 + [whole(up)],
        out_specs=pl.BlockSpec((2, 24, 4608), lambda i: (i, 0, 0)),
        out_shape=jax.ShapeDtypeStruct((2 * steps, 24, 4608), BF),
        scratch_shapes=[pltpu.VMEM((3, 288, 128), F32)],
        compiler_params=params(32),
        cost_estimate=pl.CostEstimate(flops=10**11, bytes_accessed=6 * 10**6, transcendentals=0),
    )(done_west, done_east, *quarters, up)


def passed_along(block, axis, distance):
    n = lax.axis_size(axis)
    return lax.ppermute(block, axis, [((i - distance) % n, i) for i in range(n)])


def packed_call(kernel, packed, shape, dtype):
    return pl.pallas_call(
        kernel,
        out_shape=jax.ShapeDtypeStruct(shape, dtype),
        in_specs=[pl.BlockSpec(memory_space=pltpu.VMEM)],
        out_specs=pl.BlockSpec(memory_space=pltpu.VMEM),
        compiler_params=pltpu.CompilerParams(vmem_limit_bytes=16 * MIB),
    )(packed)


def reduce_everywhere(packed, meanwhile):
    axes = ("lon", "lat")
    if lax.axis_size("lon") * lax.axis_size("lat") != packed.shape[0]:
        packed = lax.psum(packed.astype(F32), axes).astype(BF)
    else:
        parts = lax.all_to_all(packed, axes, 0, 0)
        parts, meanwhile = lax.optimization_barrier((parts, meanwhile))
        packed = lax.all_to_all(packed_call(sum_kernel, parts, packed.shape, BF), axes, 0, 0)
    return packed_call(unpack_kernel, packed, (384, 768), F32), meanwhile


def shards(
    field, cotangent,
    fine_gain_a, fine_qkv, fine_out, fine_bias, fine_gain_b, fine_in, fine_back,
    merge_gain, merge_weight,
    coarse_gain_a, coarse_qkv, coarse_out, coarse_bias, coarse_gain_b, coarse_in, coarse_back,
    up_weight,
):
    width = fine_qkv.shape[0]
    half = 6 * width
    halo = passed_along(field[:, :, :half], "lon", -1)
    fine_consts = (
        fine_bias.reshape(fine_bias.shape[0], fine_bias.shape[1], 144, 144),
        fine_gain_a, fine_qkv, fine_out, fine_gain_b, fine_in, fine_back, merge_gain, merge_weight,
    )
    coarse_consts = (
        coarse_bias.reshape(coarse_bias.shape[0], coarse_bias.shape[1], 144, 144),
        coarse_gain_a, coarse_qkv, coarse_out, coarse_gain_b, coarse_in, coarse_back,
    )
    a_left, a_right, ca_left, ca_right = fine_call(field, 1, field, 2, fine_consts)
    halo, ca_left, a_left = lax.optimization_barrier((halo, ca_left, a_left))
    ca_next = passed_along(ca_left, "lon", -1)
    cot_first, a_left = lax.optimization_barrier((cotangent[:, :, : 2 * half], a_left))
    cot_next = passed_along(cot_first, "lon", -1)
    b_left, b_right, cb_left, cb_right = fine_call(field, 3, halo, 0, fine_consts)
    b_prev = passed_along(b_right, "lon", 1)
    done_own, done_next, packed = coarse_call((ca_right, cb_left, cb_right, ca_next), cotangent, cot_next, coarse_consts)
    done_prev = passed_along(done_next, "lon", 1)
    packed, b_prev = lax.optimization_barrier((packed, b_prev))
    output = final_call(done_prev, done_own, (b_prev, a_left, a_right, b_left), up_weight)
    up_grad, output = reduce_everywhere(packed, output)
    return output, up_grad


def solution(mesh):
    lat = P(None, "lat", None)
    split = P(None, "lat", "lon")
    return jax.shard_map(
        shards,
        mesh=mesh,
        in_specs=(split, split, P(), P(), P(), lat) + (P(),) * 8 + (lat,) + (P(),) * 4,
        out_specs=(split, P()),
        check_vma=False,
    )
```

```python
import functools
import jax
import jax.numpy as jnp
from jax import lax
from jax.experimental import pallas as pl
from jax.experimental.pallas import tpu as pltpu
from jax.sharding import PartitionSpec as P

BF = jnp.bfloat16
F32 = jnp.float32
NN = (((1,), (0,)), ((), ()))
NT = (((1,), (1,)), ((), ()))
TN = (((0,), (0,)), ((), ()))
LOG2E = 1.4426950408889634
HD = 32
UNITS = 2
LEAD = 0
MIB = 1024 * 1024


def mm(a, b, dims=NN):
    return lax.dot_general(a, b, dims, preferred_element_type=F32)


def row(ref):
    return ref[...].reshape(1, ref.shape[0])


def layer_norm(value, gain):
    center = value - jnp.mean(value, axis=-1, keepdims=True)
    spread = jnp.mean(center * center, axis=-1, keepdims=True)
    return center * lax.rsqrt(spread + 1e-05) * gain


def scaled_bias(bias_ref, table_ref, heads):
    count = bias_ref.shape[1]
    stack = 8 // count
    lane = lax.broadcasted_iota(jnp.int32, (8, 128), 1)

    def eight(m, carry):
        for g in range(heads // stack):
            tiles = []
            for i in range(9):
                at = pl.multiple_of(m * 1152 + i * 128, 128)
                parts = [bias_ref[g * stack + k, :, pl.ds(at, 128)].astype(F32) for k in range(stack)]
                tiles.append(jnp.concatenate(parts, axis=0) * LOG2E)
            for j in range(8):
                main, tail = tiles[j], tiles[j + 1]
                if j > 0:
                    main = pltpu.roll(jnp.where(lane >= 16 * j, main, tail), 128 - 16 * j, axis=1)
                    tail = pltpu.roll(tail, 128 - 16 * j, axis=1)
                rows = pl.ds(g * 8 * 144 + m * 8 + j, 8, stride=144)
                table_ref[0, rows, :] = main
                table_ref[1, rows, :] = tail
        return carry

    lax.fori_loop(0, 18, eight, 0)


def put_rows(ref, at, value):
    for t in range(value.shape[1] // 128):
        ref[t, at : at + value.shape[0], :] = value[:, t * 128 : (t + 1) * 128]


def get_rows(ref, at, count):
    return jnp.concatenate([ref[t, at : at + count, :] for t in range(ref.shape[0])], axis=1)


def get_every_other(ref, at, count):
    return jnp.concatenate([ref[t, pl.ds(at, count, stride=2), :] for t in range(ref.shape[0])], axis=1)


def put_every_other(ref, at, value):
    for t in range(ref.shape[0]):
        ref[t, pl.ds(at, value.shape[0], stride=2), :] = value[:, t * 128 : (t + 1) * 128]


def tiled(value):
    short = -value.shape[1] % 128
    if short:
        value = jnp.concatenate([value, jnp.zeros((value.shape[0], short), value.dtype)], axis=1)
    return value


def window_block(result, v, ga, wq, wk, wv, w_out, table_ref, gb, w_in, w_back, mixed_ref):
    tokens, width = v.shape
    heads = width // HD
    aw = layer_norm(v, ga).astype(BF)
    yield
    q_all = (mm(aw, wq) * (LOG2E * HD**-0.5)).astype(BF)
    k_all = mm(aw, wk).astype(BF)
    v_all = mm(aw, wv).astype(BF)
    yield
    lane = lax.broadcasted_iota(jnp.int32, (144, 128), 1)
    ones = jnp.ones((144, 128), BF)
    for w in range(tokens // 144):
        rows = slice(w * 144, (w + 1) * 144)
        for t in range(-(-width // 128)):
            lanes = slice(t * 128, t * 128 + 128)
            total = jnp.zeros((144, 128), F32)
            count = jnp.ones((144, 128), F32)
            q, k = q_all[rows, lanes], k_all[rows, lanes]
            values = jnp.concatenate([v_all[rows, lanes], ones], axis=1)
            for j in range(min(4, heads - 4 * t)):
                mine = (lane >= j * HD) & (lane < j * HD + HD)
                first = ((4 * t + j) * (tokens // 144) + w) * 144
                at = slice(first, first + 144)
                bias = jnp.concatenate([table_ref[0, at, :], table_ref[1, at, :16]], axis=1)
                s = mm(jnp.where(mine, q, jnp.zeros_like(q)), k, NT) + bias
                p = jnp.exp2(s - jnp.max(s, axis=1, keepdims=True)).astype(BF)
                o = mm(p, values)
                total = jnp.where(mine, o[:, :128], total)
                count = jnp.where(mine, o[:, 128:], count)
            mixed_ref[rows, lanes] = (total / count).astype(BF)
            yield
    r = v + mm(mixed_ref[:, :width], w_out)
    m = layer_norm(r, gb).astype(BF)
    yield
    u = jax.nn.gelu(mm(m, w_in)).astype(BF)
    yield
    result.append((r + mm(u, w_back, NT)).astype(BF))
    yield


def interleave(streams, lead):
    waiting = list(streams)
    for _ in range(lead):
        next(waiting[0], None)
    while waiting:
        waiting = [g for g in waiting if next(g, g) is not g]


def fine_moves():
    for l in range(2):
        for row in range(24):
            for c in range(2):
                yield l * 288 + c * 144 + row, (row // 6) * 144 + l * 72 + (row % 6) * 12 + c


def fine_kernel(
    left_ref, right_ref, bias_ref, ga_ref, wqkv_ref, wo_ref, gb_ref,
    wi_ref, wb_ref, mg_ref, mw_ref,
    out_left, out_right, coarse_left, coarse_right, nat_ref, win_ref, table_ref, mixed_ref, proj_ref,
):
    heads = bias_ref.shape[0]

    @pl.when(pl.program_id(0) == 0)
    def _():
        scaled_bias(bias_ref, table_ref, heads)
        width = wo_ref.shape[0]
        proj_ref[...] = jnp.zeros_like(proj_ref)
        for i in range(3):
            proj_ref[i, :, :width] = wqkv_ref[:, i * width : (i + 1) * width]

    units = left_ref.shape[0] // 2
    interleave(
        [
            fine_unit(
                u, (left_ref, right_ref), ga_ref, proj_ref, wo_ref, gb_ref, wi_ref, wb_ref, mg_ref, mw_ref,
                (out_left, out_right), coarse_left, coarse_right, nat_ref.at[u], win_ref.at[u], table_ref, mixed_ref.at[u],
            )
            for u in range(units)
        ],
        LEAD if units > 1 else 0,
    )


def fine_unit(
    u, halves, ga_ref, proj_ref, wo_ref, gb_ref, wi_ref, wb_ref, mg_ref, mw_ref,
    outs, coarse_left, coarse_right, nat_ref, win_ref, table_ref, mixed_ref,
):
    width = wo_ref.shape[0]
    pair = 2 * width
    for l in range(2):
        for s in range(2):
            for p in range(3):
                at = l * 288 + (s * 3 + p) * 24
                x = halves[s][2 * u + l, :, p * pair : (p + 1) * pair].astype(F32)
                put_rows(nat_ref, at, x[:, :256])
                put_rows(nat_ref, at + 144, pltpu.roll(x[:, 128:], 192, axis=1))
    for src, dst in fine_moves():
        for t in range(2):
            win_ref[t, pl.ds(dst, 6, stride=2), :] = nat_ref[t, pl.ds(src, 6, stride=24), :]
    v = get_rows(win_ref, 0, 576)[:, :width]
    yield
    result = []
    yield from window_block(
        result, v, row(ga_ref), proj_ref[0], proj_ref[1], proj_ref[2], wo_ref[...],
        table_ref, row(gb_ref), wi_ref[...], wb_ref[...], mixed_ref,
    )
    done = result[0].astype(F32)
    put_rows(win_ref, 0, tiled(done))
    for src, dst in fine_moves():
        for t in range(2):
            nat_ref[t, pl.ds(src, 6, stride=24), :] = win_ref[t, pl.ds(dst, 6, stride=2), :]
    yield
    quarter = []
    for r in range(2):
        for c in range(2):
            quarter.append(
                jnp.concatenate(
                    [get_every_other(nat_ref, l * 288 + c * 144 + r, 72)[:, :width] for l in range(2)], axis=0
                )
            )
    mean = sum(jnp.sum(x, axis=-1, keepdims=True) for x in quarter) * (1.0 / (4 * width))
    center = [x - mean for x in quarter]
    spread = sum(jnp.sum(x * x, axis=-1, keepdims=True) for x in center) * (1.0 / (4 * width))
    scale = lax.rsqrt(spread + 1e-05)
    gains = row(mg_ref)
    coarse = 0.0
    for i in range(4):
        n = (center[i] * scale * gains[:, i * width : (i + 1) * width]).astype(BF)
        coarse = coarse + mm(n, mw_ref[i * width : (i + 1) * width])
    for l in range(2):
        coarse_left[u, l] = coarse[l * 72 : l * 72 + 36].astype(BF)
        coarse_right[u, l] = coarse[l * 72 + 36 : l * 72 + 72].astype(BF)
    yield
    low = lax.broadcasted_iota(jnp.int32, (24, 128), 1) < 64
    for l in range(2):
        for s in range(2):
            for p in range(3):
                at = l * 288 + (s * 3 + p) * 24
                even = get_rows(nat_ref, at, 24)
                odd = pltpu.roll(get_rows(nat_ref, at + 144, 24), 64, axis=1)
                middle = jnp.where(low, even[:, 128:], odd[:, :128])
                outs[s][2 * u + l, :, p * pair : (p + 1) * pair] = jnp.concatenate(
                    [even[:, :128], middle, odd[:, 128:]], axis=1
                ).astype(BF)


def coarse_kernel(
    g0, g1, g2, g3, cot_ref, cot_next_ref, bias_ref, ga_ref, wqkv_ref, wo_ref, gb_ref,
    wi_ref, wb_ref,
    done_own, done_next, packed_ref, nat_ref, win_ref, table_ref, mixed_ref, grad_ref,
):
    heads = bias_ref.shape[0]

    @pl.when(pl.program_id(0) == 0)
    def _():
        scaled_bias(bias_ref, table_ref, heads)
        grad_ref[...] = jnp.zeros_like(grad_ref)

    units = g0.shape[0]
    interleave(
        [
            coarse_unit(
                u, (g0, g1, g2, g3), cot_ref, cot_next_ref, ga_ref, wqkv_ref, wo_ref, gb_ref, wi_ref, wb_ref,
                done_own, done_next, grad_ref, nat_ref.at[u], win_ref.at[u], table_ref, mixed_ref.at[u],
            )
            for u in range(units)
        ],
        LEAD if units > 1 else 0,
    )

    @pl.when(pl.program_id(0) == pl.num_programs(0) - 1)
    def _():
        for j in range(128):
            t, b = divmod(j, 24)
            packed_ref[j, :16, :] = grad_ref[b * 16 : b * 16 + 16, t * 128 : (t + 1) * 128].astype(BF)
            packed_ref[j, 16:, :] = grad_ref[128 + 2 * j : 130 + 2 * j, 640:].astype(BF)


def sum_kernel(in_ref, out_ref):
    total = in_ref[0].astype(F32)
    for j in range(1, 128):
        total = total + in_ref[j].astype(F32)
    total = total.astype(BF)
    for j in range(128):
        out_ref[j] = total


def unpack_kernel(in_ref, out_ref):
    for j in range(128):
        t, b = divmod(j, 24)
        out_ref[b * 16 : b * 16 + 16, t * 128 : (t + 1) * 128] = in_ref[j, :16, :].astype(F32)
        out_ref[128 + 2 * j : 130 + 2 * j, 640:] = in_ref[j, 16:, :].astype(F32)


def coarse_unit(
    u, groups, cot_ref, cot_next_ref, ga_ref, wqkv_ref, wo_ref, gb_ref, wi_ref, wb_ref,
    done_own, done_next, grad_ref, nat_ref, win_ref, table_ref, mixed_ref,
):
    width = wo_ref.shape[0]
    for l in range(2):
        for i, g in enumerate(groups):
            put_rows(nat_ref, l * 144 + i * 36, g[u, l].astype(F32))
    moves = [(l * 144 + row, (row // 6) * 144 + l * 72 + (row % 6) * 12) for l in range(2) for row in range(12)]
    for src, dst in moves:
        for t in range(3):
            win_ref[t, dst : dst + 12, :] = nat_ref[t, pl.ds(src, 12, stride=12), :]
    yield
    result = []
    yield from window_block(
        result, get_rows(win_ref, 0, 288), row(ga_ref), wqkv_ref[:, :width], wqkv_ref[:, width : 2 * width],
        wqkv_ref[:, 2 * width :], wo_ref[...],
        table_ref, row(gb_ref), wi_ref[...], wb_ref[...], mixed_ref,
    )
    done = result[0]
    put_rows(win_ref, 0, done.astype(F32))
    for src, dst in moves:
        for t in range(3):
            nat_ref[t, pl.ds(src, 12, stride=12), :] = win_ref[t, dst : dst + 12, :]
    yield
    for half, ref, out in ((0, cot_ref, done_own), (1, cot_next_ref, done_next)):
        tokens = jnp.concatenate([get_rows(nat_ref, l * 144 + half * 72, 72) for l in range(2)], axis=0).astype(BF)
        out[u] = tokens
        for l in range(2):
            for c in range(6):
                put_rows(win_ref, (l * 6 + c) * 24, ref[2 * u + l, :, c * width : (c + 1) * width].astype(F32))
        for r in range(2):
            x = get_every_other(win_ref, r, 144).astype(BF)
            grad_ref[:, r * width : (r + 1) * width] += mm(tokens, x, TN)
        yield


def final_kernel(done_west, done_east, set0, set1, set2, set3, up_ref, out_ref, rows_ref):
    width = done_west.shape[2]
    halves = (set0, set1, set2, set3)
    for e, done_ref in enumerate((done_west, done_east)):
        raised = mm(done_ref[0], up_ref[...])
        for r in range(2):
            put_every_other(rows_ref, r, raised[:, r * width : (r + 1) * width])
        for l in range(2):
            for c in range(6):
                base = halves[2 * e + c // 3][l, :, (c % 3) * width : (c % 3 + 1) * width]
                total = base.astype(F32) + get_rows(rows_ref, (l * 6 + c) * 24, 24)
                out_ref[l, :, (e * 6 + c) * width : (e * 6 + c + 1) * width] = total.astype(BF)


def whole(a):
    return pl.BlockSpec(a.shape, lambda i: (0,) * a.ndim)


def params(mib):
    return pltpu.CompilerParams(vmem_limit_bytes=mib * MIB, dimension_semantics=("arbitrary",))


def fine_call(left, left_at, right, right_at, consts):
    levels, rows, _ = left.shape
    half = 1152
    steps = levels // (2 * UNITS)

    def spec(at):
        return pl.BlockSpec((2 * UNITS, rows, half), lambda i: (i, 0, at))

    cspec = pl.BlockSpec((UNITS, 2, 36, 384), lambda i: (i, 0, 0, 0))
    return pl.pallas_call(
        fine_kernel,
        grid=(steps,),
        in_specs=[spec(left_at), spec(right_at)] + [whole(c) for c in consts],
        out_specs=[spec(0), spec(0), cspec, cspec],
        out_shape=[jax.ShapeDtypeStruct((levels, rows, half), BF)] * 2
        + [jax.ShapeDtypeStruct((steps * UNITS, 2, 36, 384), BF)] * 2,
        scratch_shapes=[
            pltpu.VMEM((UNITS, 2, 576, 128), F32),
            pltpu.VMEM((UNITS, 2, 576, 128), F32),
            pltpu.VMEM((2, 24 * 144, 128), F32),
            pltpu.VMEM((UNITS, 576, 256), BF),
            pltpu.VMEM((3, 192, 256), BF),
        ],
        compiler_params=params(56),
        cost_estimate=pl.CostEstimate(flops=3 * 10**9, bytes_accessed=6 * 10**6, transcendentals=10**6),
    )(left, right, *consts)


def coarse_call(groups, cot, cot_next, consts):
    steps = groups[0].shape[0] // UNITS
    gspec = pl.BlockSpec((UNITS, 2, 36, 384), lambda i: (i, 0, 0, 0))
    dspec = pl.BlockSpec((UNITS, 144, 384), lambda i: (i, 0, 0))
    return pl.pallas_call(
        coarse_kernel,
        grid=(steps,),
        in_specs=[gspec] * 4
        + [pl.BlockSpec((2 * UNITS, 24, 2304), lambda i: (i, 0, 1)), pl.BlockSpec((2 * UNITS, 24, 2304), lambda i: (i, 0, 0))]
        + [whole(c) for c in consts],
        out_specs=[dspec, dspec, pl.BlockSpec((128, 18, 128), lambda i: (0, 0, 0))],
        out_shape=[jax.ShapeDtypeStruct((steps * UNITS, 144, 384), BF)] * 2
        + [jax.ShapeDtypeStruct((128, 18, 128), BF)],
        scratch_shapes=[
            pltpu.VMEM((UNITS, 3, 288, 128), F32),
            pltpu.VMEM((UNITS, 3, 288, 128), F32),
            pltpu.VMEM((2, 24 * 144, 128), F32),
            pltpu.VMEM((UNITS, 288, 384), BF),
            pltpu.VMEM((384, 768), F32),
        ],
        compiler_params=params(56),
        cost_estimate=pl.CostEstimate(flops=5 * 10**9, bytes_accessed=8 * 10**6, transcendentals=10**6),
    )(*groups, cot, cot_next, *consts)


def final_call(done_west, done_east, quarters, up):
    steps = done_west.shape[0]
    dspec = pl.BlockSpec((1, 144, 384), lambda i: (i, 0, 0))
    sspec = pl.BlockSpec((2, 24, 1152), lambda i: (i, 0, 0))
    return pl.pallas_call(
        final_kernel,
        grid=(steps,),
        in_specs=[dspec] * 2 + [sspec] * 4 + [whole(up)],
        out_specs=pl.BlockSpec((2, 24, 4608), lambda i: (i, 0, 0)),
        out_shape=jax.ShapeDtypeStruct((2 * steps, 24, 4608), BF),
        scratch_shapes=[pltpu.VMEM((3, 288, 128), F32)],
        compiler_params=params(32),
        cost_estimate=pl.CostEstimate(flops=10**11, bytes_accessed=6 * 10**6, transcendentals=0),
    )(done_west, done_east, *quarters, up)


def passed_along(block, axis, distance):
    n = lax.axis_size(axis)
    return lax.ppermute(block, axis, [((i - distance) % n, i) for i in range(n)])


def packed_call(kernel, packed, shape, dtype):
    return pl.pallas_call(
        kernel,
        out_shape=jax.ShapeDtypeStruct(shape, dtype),
        in_specs=[pl.BlockSpec(memory_space=pltpu.VMEM)],
        out_specs=pl.BlockSpec(memory_space=pltpu.VMEM),
        compiler_params=pltpu.CompilerParams(vmem_limit_bytes=16 * MIB),
    )(packed)


def reduce_everywhere(packed, meanwhile):
    axes = ("lon", "lat")
    if lax.axis_size("lon") * lax.axis_size("lat") != packed.shape[0]:
        packed = lax.psum(packed.astype(F32), axes).astype(BF)
    else:
        parts = lax.all_to_all(packed, axes, 0, 0)
        parts, meanwhile = lax.optimization_barrier((parts, meanwhile))
        packed = lax.all_to_all(packed_call(sum_kernel, parts, packed.shape, BF), axes, 0, 0)
    return packed_call(unpack_kernel, packed, (384, 768), F32), meanwhile


def shards(
    field, cotangent,
    fine_gain_a, fine_qkv, fine_out, fine_bias, fine_gain_b, fine_in, fine_back,
    merge_gain, merge_weight,
    coarse_gain_a, coarse_qkv, coarse_out, coarse_bias, coarse_gain_b, coarse_in, coarse_back,
    up_weight,
):
    width = fine_qkv.shape[0]
    half = 6 * width
    halo = passed_along(field[:, :, :half], "lon", -1)
    fine_consts = (
        fine_bias,
        fine_gain_a, fine_qkv, fine_out, fine_gain_b, fine_in, fine_back, merge_gain, merge_weight,
    )
    coarse_consts = (
        coarse_bias,
        coarse_gain_a, coarse_qkv, coarse_out, coarse_gain_b, coarse_in, coarse_back,
    )
    a_left, a_right, ca_left, ca_right = fine_call(field, 1, field, 2, fine_consts)
    halo, ca_left, a_left = lax.optimization_barrier((halo, ca_left, a_left))
    ca_next = passed_along(ca_left, "lon", -1)
    cot_first, a_left = lax.optimization_barrier((cotangent[:, :, : 2 * half], a_left))
    cot_next = passed_along(cot_first, "lon", -1)
    b_left, b_right, cb_left, cb_right = fine_call(field, 3, halo, 0, fine_consts)
    b_prev = passed_along(b_right, "lon", 1)
    done_own, done_next, packed = coarse_call((ca_right, cb_left, cb_right, ca_next), cotangent, cot_next, coarse_consts)
    done_prev = passed_along(done_next, "lon", 1)
    packed, b_prev = lax.optimization_barrier((packed, b_prev))
    output = final_call(done_prev, done_own, (b_prev, a_left, a_right, b_left), up_weight)
    up_grad, output = reduce_everywhere(packed, output)
    return output, up_grad


def solution(mesh):
    lat = P(None, "lat", None)
    split = P(None, "lat", "lon")
    return jax.shard_map(
        shards,
        mesh=mesh,
        in_specs=(split, split, P(), P(), P(), lat) + (P(),) * 8 + (lat,) + (P(),) * 4,
        out_specs=(split, P()),
        check_vma=False,
    )
```

```python
import functools
import jax
import jax.numpy as jnp
from jax import lax
from jax.experimental import pallas as pl
from jax.experimental.pallas import tpu as pltpu
from jax.sharding import PartitionSpec as P

BF = jnp.bfloat16
F32 = jnp.float32
NN = (((1,), (0,)), ((), ()))
NT = (((1,), (1,)), ((), ()))
TN = (((0,), (0,)), ((), ()))
LOG2E = 1.4426950408889634
HD = 32
UNITS = 2
LEAD = 0
MIB = 1024 * 1024


def mm(a, b, dims=NN):
    return lax.dot_general(a, b, dims, preferred_element_type=F32)


def row(ref):
    return ref[...].reshape(1, ref.shape[0])


def layer_norm(value, gain):
    center = value - jnp.mean(value, axis=-1, keepdims=True)
    spread = jnp.mean(center * center, axis=-1, keepdims=True)
    return center * lax.rsqrt(spread + 1e-05) * gain


def scaled_bias(bias_ref, table_ref, heads):
    count = bias_ref.shape[1]
    stack = 8 // count
    lane = lax.broadcasted_iota(jnp.int32, (8, 128), 1)

    def eight(m, carry):
        for g in range(heads // stack):
            tiles = []
            for i in range(9):
                at = pl.multiple_of(m * 1152 + i * 128, 128)
                parts = [bias_ref[g * stack + k, :, pl.ds(at, 128)].astype(F32) for k in range(stack)]
                tiles.append(jnp.concatenate(parts, axis=0) * LOG2E)
            for j in range(8):
                main, tail = tiles[j], tiles[j + 1]
                if j > 0:
                    main = pltpu.roll(jnp.where(lane >= 16 * j, main, tail), 128 - 16 * j, axis=1)
                    tail = pltpu.roll(tail, 128 - 16 * j, axis=1)
                rows = pl.ds(g * 8 * 144 + m * 8 + j, 8, stride=144)
                table_ref[0, rows, :] = main
                table_ref[1, rows, :] = tail
        return carry

    lax.fori_loop(0, 18, eight, 0)


def put_rows(ref, at, value):
    for t in range(value.shape[1] // 128):
        ref[t, at : at + value.shape[0], :] = value[:, t * 128 : (t + 1) * 128]


def get_rows(ref, at, count):
    return jnp.concatenate([ref[t, at : at + count, :] for t in range(ref.shape[0])], axis=1)


def get_every_other(ref, at, count):
    return jnp.concatenate([ref[t, pl.ds(at, count, stride=2), :] for t in range(ref.shape[0])], axis=1)


def put_every_other(ref, at, value):
    for t in range(ref.shape[0]):
        ref[t, pl.ds(at, value.shape[0], stride=2), :] = value[:, t * 128 : (t + 1) * 128]


def tiled(value):
    short = -value.shape[1] % 128
    if short:
        value = jnp.concatenate([value, jnp.zeros((value.shape[0], short), value.dtype)], axis=1)
    return value


def window_block(result, v, ga, wq, wk, wv, w_out, table_ref, gb, w_in, w_back, mixed_ref):
    tokens, width = v.shape
    heads = width // HD
    aw = layer_norm(v, ga).astype(BF)
    yield
    q_all = (mm(aw, wq) * (LOG2E * HD**-0.5)).astype(BF)
    k_all = mm(aw, wk).astype(BF)
    v_all = mm(aw, wv).astype(BF)
    yield
    lane = lax.broadcasted_iota(jnp.int32, (144, 128), 1)
    ones = jnp.ones((144, 128), BF)
    for w in range(tokens // 144):
        rows = slice(w * 144, (w + 1) * 144)
        for t in range(-(-width // 128)):
            lanes = slice(t * 128, t * 128 + 128)
            total = jnp.zeros((144, 128), F32)
            count = jnp.ones((144, 128), F32)
            q, k = q_all[rows, lanes], k_all[rows, lanes]
            values = jnp.concatenate([v_all[rows, lanes], ones], axis=1)
            for j in range(min(4, heads - 4 * t)):
                mine = (lane >= j * HD) & (lane < j * HD + HD)
                first = ((4 * t + j) * (tokens // 144) + w) * 144
                at = slice(first, first + 144)
                bias = jnp.concatenate([table_ref[0, at, :], table_ref[1, at, :16]], axis=1)
                s = mm(jnp.where(mine, q, jnp.zeros_like(q)), k, NT) + bias
                p = jnp.exp2(s - jnp.max(s, axis=1, keepdims=True)).astype(BF)
                o = mm(p, values)
                total = jnp.where(mine, o[:, :128], total)
                count = jnp.where(mine, o[:, 128:], count)
            mixed_ref[rows, lanes] = (total / count).astype(BF)
            yield
    r = v + mm(mixed_ref[:, :width], w_out)
    m = layer_norm(r, gb).astype(BF)
    yield
    u = jax.nn.gelu(mm(m, w_in)).astype(BF)
    yield
    result.append((r + mm(u, w_back, NT)).astype(BF))
    yield


def interleave(streams, lead):
    waiting = list(streams)
    for _ in range(lead):
        next(waiting[0], None)
    while waiting:
        waiting = [g for g in waiting if next(g, g) is not g]


def fine_moves():
    for l in range(2):
        for row in range(24):
            for c in range(2):
                yield l * 288 + c * 144 + row, (row // 6) * 144 + l * 72 + (row % 6) * 12 + c


def fine_kernel(
    left_ref, right_ref, bias_ref, ga_ref, wqkv_ref, wo_ref, gb_ref,
    wi_ref, wb_ref, mg_ref, mw_ref,
    out_left, out_right, coarse_left, coarse_right, nat_ref, win_ref, table_ref, mixed_ref, proj_ref,
):
    heads = bias_ref.shape[0]

    @pl.when(pl.program_id(0) == 0)
    def _():
        scaled_bias(bias_ref, table_ref, heads)
        width = wo_ref.shape[0]
        proj_ref[...] = jnp.zeros_like(proj_ref)
        for i in range(3):
            proj_ref[i, :, :width] = wqkv_ref[:, i * width : (i + 1) * width]

    units = left_ref.shape[0] // 2
    interleave(
        [
            fine_unit(
                u, (left_ref, right_ref), ga_ref, proj_ref, wo_ref, gb_ref, wi_ref, wb_ref, mg_ref, mw_ref,
                (out_left, out_right), coarse_left, coarse_right, nat_ref.at[u], win_ref.at[u], table_ref, mixed_ref.at[u],
            )
            for u in range(units)
        ],
        LEAD if units > 1 else 0,
    )


def fine_unit(
    u, halves, ga_ref, proj_ref, wo_ref, gb_ref, wi_ref, wb_ref, mg_ref, mw_ref,
    outs, coarse_left, coarse_right, nat_ref, win_ref, table_ref, mixed_ref,
):
    width = wo_ref.shape[0]
    pair = 2 * width
    for l in range(2):
        for s in range(2):
            for p in range(3):
                at = l * 288 + (s * 3 + p) * 24
                x = halves[s][2 * u + l, :, p * pair : (p + 1) * pair].astype(F32)
                put_rows(nat_ref, at, x[:, :256])
                put_rows(nat_ref, at + 144, pltpu.roll(x[:, 128:], 192, axis=1))
    for src, dst in fine_moves():
        for t in range(2):
            win_ref[t, pl.ds(dst, 6, stride=2), :] = nat_ref[t, pl.ds(src, 6, stride=24), :]
    v = get_rows(win_ref, 0, 576)[:, :width]
    yield
    result = []
    yield from window_block(
        result, v, row(ga_ref), proj_ref[0], proj_ref[1], proj_ref[2], wo_ref[...],
        table_ref, row(gb_ref), wi_ref[...], wb_ref[...], mixed_ref,
    )
    done = result[0].astype(F32)
    put_rows(win_ref, 0, tiled(done))
    for src, dst in fine_moves():
        for t in range(2):
            nat_ref[t, pl.ds(src, 6, stride=24), :] = win_ref[t, pl.ds(dst, 6, stride=2), :]
    yield
    quarter = []
    for r in range(2):
        for c in range(2):
            quarter.append(
                jnp.concatenate(
                    [get_every_other(nat_ref, l * 288 + c * 144 + r, 72)[:, :width] for l in range(2)], axis=0
                )
            )
    mean = sum(jnp.sum(x, axis=-1, keepdims=True) for x in quarter) * (1.0 / (4 * width))
    center = [x - mean for x in quarter]
    spread = sum(jnp.sum(x * x, axis=-1, keepdims=True) for x in center) * (1.0 / (4 * width))
    scale = lax.rsqrt(spread + 1e-05)
    gains = row(mg_ref)
    coarse = 0.0
    for i in range(4):
        n = (center[i] * scale * gains[:, i * width : (i + 1) * width]).astype(BF)
        coarse = coarse + mm(n, mw_ref[i * width : (i + 1) * width])
    for l in range(2):
        coarse_left[u, l] = coarse[l * 72 : l * 72 + 36].astype(BF)
        coarse_right[u, l] = coarse[l * 72 + 36 : l * 72 + 72].astype(BF)
    yield
    low = lax.broadcasted_iota(jnp.int32, (24, 128), 1) < 64
    for l in range(2):
        for s in range(2):
            for p in range(3):
                at = l * 288 + (s * 3 + p) * 24
                even = get_rows(nat_ref, at, 24)
                odd = pltpu.roll(get_rows(nat_ref, at + 144, 24), 64, axis=1)
                middle = jnp.where(low, even[:, 128:], odd[:, :128])
                outs[s][2 * u + l, :, p * pair : (p + 1) * pair] = jnp.concatenate(
                    [even[:, :128], middle, odd[:, 128:]], axis=1
                ).astype(BF)


def coarse_kernel(
    g0, g1, g2, g3, cot_ref, cot_near_ref, cot_far_ref, bias_ref, ga_ref, wqkv_ref, wo_ref, gb_ref,
    wi_ref, wb_ref,
    done_own, done_next, packed_ref, nat_ref, win_ref, table_ref, mixed_ref, grad_ref,
):
    heads = bias_ref.shape[0]

    @pl.when(pl.program_id(0) == 0)
    def _():
        scaled_bias(bias_ref, table_ref, heads)
        grad_ref[...] = jnp.zeros_like(grad_ref)

    units = g0.shape[0]
    interleave(
        [
            coarse_unit(
                u, (g0, g1, g2, g3), cot_ref, cot_near_ref, cot_far_ref, ga_ref, wqkv_ref, wo_ref, gb_ref, wi_ref, wb_ref,
                done_own, done_next, grad_ref, nat_ref.at[u], win_ref.at[u], table_ref, mixed_ref.at[u],
            )
            for u in range(units)
        ],
        LEAD if units > 1 else 0,
    )

    @pl.when(pl.program_id(0) == pl.num_programs(0) - 1)
    def _():
        for j in range(128):
            t, b = divmod(j, 24)
            packed_ref[j, :16, :] = grad_ref[b * 16 : b * 16 + 16, t * 128 : (t + 1) * 128].astype(BF)
            packed_ref[j, 16:, :] = grad_ref[128 + 2 * j : 130 + 2 * j, 640:].astype(BF)


def sum_kernel(in_ref, out_ref):
    total = in_ref[0].astype(F32)
    for j in range(1, 128):
        total = total + in_ref[j].astype(F32)
    total = total.astype(BF)
    for j in range(128):
        out_ref[j] = total


def unpack_kernel(in_ref, out_ref):
    for j in range(128):
        t, b = divmod(j, 24)
        out_ref[b * 16 : b * 16 + 16, t * 128 : (t + 1) * 128] = in_ref[j, :16, :].astype(F32)
        out_ref[128 + 2 * j : 130 + 2 * j, 640:] = in_ref[j, 16:, :].astype(F32)


def coarse_unit(
    u, groups, cot_ref, cot_near_ref, cot_far_ref, ga_ref, wqkv_ref, wo_ref, gb_ref, wi_ref, wb_ref,
    done_own, done_next, grad_ref, nat_ref, win_ref, table_ref, mixed_ref,
):
    width = wo_ref.shape[0]
    for l in range(2):
        for i, g in enumerate(groups):
            put_rows(nat_ref, l * 144 + i * 36, g[u, l].astype(F32))
    moves = [(l * 144 + row, (row // 6) * 144 + l * 72 + (row % 6) * 12) for l in range(2) for row in range(12)]
    for src, dst in moves:
        for t in range(3):
            win_ref[t, dst : dst + 12, :] = nat_ref[t, pl.ds(src, 12, stride=12), :]
    yield
    result = []
    yield from window_block(
        result, get_rows(win_ref, 0, 288), row(ga_ref), wqkv_ref[:, :width], wqkv_ref[:, width : 2 * width],
        wqkv_ref[:, 2 * width :], wo_ref[...],
        table_ref, row(gb_ref), wi_ref[...], wb_ref[...], mixed_ref,
    )
    done = result[0]
    put_rows(win_ref, 0, done.astype(F32))
    for src, dst in moves:
        for t in range(3):
            nat_ref[t, pl.ds(src, 12, stride=12), :] = win_ref[t, dst : dst + 12, :]
    yield
    for half, out in enumerate((done_own, done_next)):
        tokens = jnp.concatenate([get_rows(nat_ref, l * 144 + half * 72, 72) for l in range(2)], axis=0).astype(BF)
        out[u] = tokens
        for l in range(2):
            for c in range(6):
                ref, at = (cot_ref, c) if half == 0 else (cot_near_ref, c) if c < 2 else (cot_far_ref, c - 2)
                put_rows(win_ref, (l * 6 + c) * 24, ref[2 * u + l, :, at * width : (at + 1) * width].astype(F32))
        for r in range(2):
            x = get_every_other(win_ref, r, 144).astype(BF)
            grad_ref[:, r * width : (r + 1) * width] += mm(tokens, x, TN)
        yield


def final_kernel(done_west, done_east, set0, set1, set2, set3, up_ref, out_ref, rows_ref):
    width = done_west.shape[2]
    halves = (set0, set1, set2, set3)
    for e, done_ref in enumerate((done_west, done_east)):
        raised = mm(done_ref[0], up_ref[...])
        for r in range(2):
            put_every_other(rows_ref, r, raised[:, r * width : (r + 1) * width])
        for l in range(2):
            for c in range(6):
                base = halves[2 * e + c // 3][l, :, (c % 3) * width : (c % 3 + 1) * width]
                total = base.astype(F32) + get_rows(rows_ref, (l * 6 + c) * 24, 24)
                out_ref[l, :, (e * 6 + c) * width : (e * 6 + c + 1) * width] = total.astype(BF)


def whole(a):
    return pl.BlockSpec(a.shape, lambda i: (0,) * a.ndim)


def params(mib):
    return pltpu.CompilerParams(vmem_limit_bytes=mib * MIB, dimension_semantics=("arbitrary",))


def fine_call(left, left_at, right, right_at, consts):
    levels, rows, _ = left.shape
    half = 1152
    steps = levels // (2 * UNITS)

    def spec(at):
        return pl.BlockSpec((2 * UNITS, rows, half), lambda i: (i, 0, at))

    cspec = pl.BlockSpec((UNITS, 2, 36, 384), lambda i: (i, 0, 0, 0))
    return pl.pallas_call(
        fine_kernel,
        grid=(steps,),
        in_specs=[spec(left_at), spec(right_at)] + [whole(c) for c in consts],
        out_specs=[spec(0), spec(0), cspec, cspec],
        out_shape=[jax.ShapeDtypeStruct((levels, rows, half), BF)] * 2
        + [jax.ShapeDtypeStruct((steps * UNITS, 2, 36, 384), BF)] * 2,
        scratch_shapes=[
            pltpu.VMEM((UNITS, 2, 576, 128), F32),
            pltpu.VMEM((UNITS, 2, 576, 128), F32),
            pltpu.VMEM((2, 24 * 144, 128), F32),
            pltpu.VMEM((UNITS, 576, 256), BF),
            pltpu.VMEM((3, 192, 256), BF),
        ],
        compiler_params=params(56),
        cost_estimate=pl.CostEstimate(flops=3 * 10**9, bytes_accessed=6 * 10**6, transcendentals=10**6),
    )(left, right, *consts)


def coarse_call(groups, cot, cot_near, cot_far, consts):
    steps = groups[0].shape[0] // UNITS
    gspec = pl.BlockSpec((UNITS, 2, 36, 384), lambda i: (i, 0, 0, 0))
    dspec = pl.BlockSpec((UNITS, 144, 384), lambda i: (i, 0, 0))
    return pl.pallas_call(
        coarse_kernel,
        grid=(steps,),
        in_specs=[gspec] * 4
        + [pl.BlockSpec((2 * UNITS, 24, 2304), lambda i: (i, 0, 1)), pl.BlockSpec((2 * UNITS, 24, 768), lambda i: (i, 0, 0)),
            pl.BlockSpec((2 * UNITS, 24, 1536), lambda i: (i, 0, 0))]
        + [whole(c) for c in consts],
        out_specs=[dspec, dspec, pl.BlockSpec((128, 18, 128), lambda i: (0, 0, 0))],
        out_shape=[jax.ShapeDtypeStruct((steps * UNITS, 144, 384), BF)] * 2
        + [jax.ShapeDtypeStruct((128, 18, 128), BF)],
        scratch_shapes=[
            pltpu.VMEM((UNITS, 3, 288, 128), F32),
            pltpu.VMEM((UNITS, 3, 288, 128), F32),
            pltpu.VMEM((2, 24 * 144, 128), F32),
            pltpu.VMEM((UNITS, 288, 384), BF),
            pltpu.VMEM((384, 768), F32),
        ],
        compiler_params=params(56),
        cost_estimate=pl.CostEstimate(flops=5 * 10**9, bytes_accessed=8 * 10**6, transcendentals=10**6),
    )(*groups, cot, cot_near, cot_far, *consts)


def final_call(done_west, done_east, quarters, up):
    steps = done_west.shape[0]
    dspec = pl.BlockSpec((1, 144, 384), lambda i: (i, 0, 0))
    sspec = pl.BlockSpec((2, 24, 1152), lambda i: (i, 0, 0))
    return pl.pallas_call(
        final_kernel,
        grid=(steps,),
        in_specs=[dspec] * 2 + [sspec] * 4 + [whole(up)],
        out_specs=pl.BlockSpec((2, 24, 4608), lambda i: (i, 0, 0)),
        out_shape=jax.ShapeDtypeStruct((2 * steps, 24, 4608), BF),
        scratch_shapes=[pltpu.VMEM((3, 288, 128), F32)],
        compiler_params=params(32),
        cost_estimate=pl.CostEstimate(flops=10**11, bytes_accessed=6 * 10**6, transcendentals=0),
    )(done_west, done_east, *quarters, up)


def passed_along(block, axis, distance):
    n = lax.axis_size(axis)
    return lax.ppermute(block, axis, [((i - distance) % n, i) for i in range(n)])


def packed_call(kernel, packed, shape, dtype):
    return pl.pallas_call(
        kernel,
        out_shape=jax.ShapeDtypeStruct(shape, dtype),
        in_specs=[pl.BlockSpec(memory_space=pltpu.VMEM)],
        out_specs=pl.BlockSpec(memory_space=pltpu.VMEM),
        compiler_params=pltpu.CompilerParams(vmem_limit_bytes=16 * MIB),
    )(packed)


def reduce_everywhere(packed, meanwhile):
    axes = ("lon", "lat")
    if lax.axis_size("lon") * lax.axis_size("lat") != packed.shape[0]:
        packed = lax.psum(packed.astype(F32), axes).astype(BF)
    else:
        parts = lax.all_to_all(packed, axes, 0, 0)
        parts, meanwhile = lax.optimization_barrier((parts, meanwhile))
        packed = lax.all_to_all(packed_call(sum_kernel, parts, packed.shape, BF), axes, 0, 0)
    return packed_call(unpack_kernel, packed, (384, 768), F32), meanwhile


def shards(
    field, cotangent,
    fine_gain_a, fine_qkv, fine_out, fine_bias, fine_gain_b, fine_in, fine_back,
    merge_gain, merge_weight,
    coarse_gain_a, coarse_qkv, coarse_out, coarse_bias, coarse_gain_b, coarse_in, coarse_back,
    up_weight,
):
    width = fine_qkv.shape[0]
    half = 6 * width
    near = 4 * width
    halo = passed_along(field[:, :, :half], "lon", -1)
    cot_near = passed_along(cotangent[:, :, :near], "lon", -1)
    fine_consts = (
        fine_bias,
        fine_gain_a, fine_qkv, fine_out, fine_gain_b, fine_in, fine_back, merge_gain, merge_weight,
    )
    coarse_consts = (
        coarse_bias,
        coarse_gain_a, coarse_qkv, coarse_out, coarse_gain_b, coarse_in, coarse_back,
    )
    a_left, a_right, ca_left, ca_right = fine_call(field, 1, field, 2, fine_consts)
    halo, cot_near, ca_left, a_left = lax.optimization_barrier((halo, cot_near, ca_left, a_left))
    ca_next = passed_along(ca_left, "lon", -1)
    cot_rest, a_left = lax.optimization_barrier((cotangent[:, :, near : 2 * half], a_left))
    cot_far = passed_along(cot_rest, "lon", -1)
    b_left, b_right, cb_left, cb_right = fine_call(field, 3, halo, 0, fine_consts)
    b_prev = passed_along(b_right, "lon", 1)
    done_own, done_next, packed = coarse_call((ca_right, cb_left, cb_right, ca_next), cotangent, cot_near, cot_far, coarse_consts)
    done_prev = passed_along(done_next, "lon", 1)
    packed, b_prev = lax.optimization_barrier((packed, b_prev))
    output = final_call(done_prev, done_own, (b_prev, a_left, a_right, b_left), up_weight)
    up_grad, output = reduce_everywhere(packed, output)
    return output, up_grad


def solution(mesh):
    lat = P(None, "lat", None)
    split = P(None, "lat", "lon")
    return jax.shard_map(
        shards,
        mesh=mesh,
        in_specs=(split, split, P(), P(), P(), lat) + (P(),) * 8 + (lat,) + (P(),) * 4,
        out_specs=(split, P()),
        check_vma=False,
    )
```

```python
import functools
import jax
import jax.numpy as jnp
from jax import lax
from jax.experimental import pallas as pl
from jax.experimental.pallas import tpu as pltpu
from jax.sharding import PartitionSpec as P

BF = jnp.bfloat16
F32 = jnp.float32
NN = (((1,), (0,)), ((), ()))
NT = (((1,), (1,)), ((), ()))
TN = (((0,), (0,)), ((), ()))
LOG2E = 1.4426950408889634
HD = 32
UNITS = 2
LEAD = 0
MIB = 1024 * 1024


def mm(a, b, dims=NN):
    return lax.dot_general(a, b, dims, preferred_element_type=F32)


def row(ref):
    return ref[...].reshape(1, ref.shape[0])


def layer_norm(value, gain):
    center = value - jnp.mean(value, axis=-1, keepdims=True)
    spread = jnp.mean(center * center, axis=-1, keepdims=True)
    return center * lax.rsqrt(spread + 1e-05) * gain


def scaled_bias(bias_ref, table_ref, heads):
    count = bias_ref.shape[1]
    stack = 8 // count
    lane = lax.broadcasted_iota(jnp.int32, (8, 128), 1)

    def eight(m, carry):
        for g in range(heads // stack):
            tiles = []
            for i in range(9):
                at = pl.multiple_of(m * 1152 + i * 128, 128)
                parts = [bias_ref[g * stack + k, :, pl.ds(at, 128)].astype(F32) for k in range(stack)]
                tiles.append(jnp.concatenate(parts, axis=0) * LOG2E)
            for j in range(8):
                main, tail = tiles[j], tiles[j + 1]
                if j > 0:
                    main = pltpu.roll(jnp.where(lane >= 16 * j, main, tail), 128 - 16 * j, axis=1)
                    tail = pltpu.roll(tail, 128 - 16 * j, axis=1)
                rows = pl.ds(g * 8 * 144 + m * 8 + j, 8, stride=144)
                table_ref[0, rows, :] = main
                table_ref[1, rows, :] = tail
        return carry

    lax.fori_loop(0, 18, eight, 0)


def put_rows(ref, at, value):
    for t in range(value.shape[1] // 128):
        ref[t, at : at + value.shape[0], :] = value[:, t * 128 : (t + 1) * 128]


def get_rows(ref, at, count):
    return jnp.concatenate([ref[t, at : at + count, :] for t in range(ref.shape[0])], axis=1)


def get_every_other(ref, at, count):
    return jnp.concatenate([ref[t, pl.ds(at, count, stride=2), :] for t in range(ref.shape[0])], axis=1)


def put_every_other(ref, at, value):
    for t in range(ref.shape[0]):
        ref[t, pl.ds(at, value.shape[0], stride=2), :] = value[:, t * 128 : (t + 1) * 128]


def tiled(value):
    short = -value.shape[1] % 128
    if short:
        value = jnp.concatenate([value, jnp.zeros((value.shape[0], short), value.dtype)], axis=1)
    return value


def window_block(result, v, ga, wq, wk, wv, w_out, table_ref, gb, w_in, w_back, mixed_ref):
    tokens, width = v.shape
    heads = width // HD
    aw = layer_norm(v, ga).astype(BF)
    yield
    q_all = (mm(aw, wq) * (LOG2E * HD**-0.5)).astype(BF)
    k_all = mm(aw, wk).astype(BF)
    v_all = mm(aw, wv).astype(BF)
    yield
    lane = lax.broadcasted_iota(jnp.int32, (144, 128), 1)
    ones = jnp.ones((144, 128), BF)
    for w in range(tokens // 144):
        rows = slice(w * 144, (w + 1) * 144)
        for t in range(-(-width // 128)):
            lanes = slice(t * 128, t * 128 + 128)
            total = jnp.zeros((144, 128), F32)
            count = jnp.ones((144, 128), F32)
            q, k = q_all[rows, lanes], k_all[rows, lanes]
            values = jnp.concatenate([v_all[rows, lanes], ones], axis=1)
            for j in range(min(4, heads - 4 * t)):
                mine = (lane >= j * HD) & (lane < j * HD + HD)
                first = ((4 * t + j) * (tokens // 144) + w) * 144
                at = slice(first, first + 144)
                bias = jnp.concatenate([table_ref[0, at, :], table_ref[1, at, :16]], axis=1)
                s = mm(jnp.where(mine, q, jnp.zeros_like(q)), k, NT) + bias
                p = jnp.exp2(s - jnp.max(s, axis=1, keepdims=True)).astype(BF)
                o = mm(p, values)
                total = jnp.where(mine, o[:, :128], total)
                count = jnp.where(mine, o[:, 128:], count)
            mixed_ref[rows, lanes] = (total / count).astype(BF)
            yield
    r = v + mm(mixed_ref[:, :width], w_out)
    m = layer_norm(r, gb).astype(BF)
    yield
    u = jax.nn.gelu(mm(m, w_in)).astype(BF)
    yield
    result.append((r + mm(u, w_back, NT)).astype(BF))
    yield


def interleave(streams, lead):
    waiting = list(streams)
    for _ in range(lead):
        next(waiting[0], None)
    while waiting:
        waiting = [g for g in waiting if next(g, g) is not g]


def fine_moves():
    for l in range(2):
        for row in range(24):
            for c in range(2):
                yield l * 288 + c * 144 + row, (row // 6) * 144 + l * 72 + (row % 6) * 12 + c


def fine_kernel(
    left_ref, right_ref, bias_ref, ga_ref, wqkv_ref, wo_ref, gb_ref,
    wi_ref, wb_ref, mg_ref, mw_ref,
    out_left, out_right, coarse_left, coarse_right, nat_ref, win_ref, table_ref, mixed_ref, proj_ref,
):
    heads = bias_ref.shape[0]

    @pl.when(pl.program_id(0) == 0)
    def _():
        scaled_bias(bias_ref, table_ref, heads)
        width = wo_ref.shape[0]
        proj_ref[...] = jnp.zeros_like(proj_ref)
        for i in range(3):
            proj_ref[i, :, :width] = wqkv_ref[:, i * width : (i + 1) * width]

    units = left_ref.shape[0] // 2
    interleave(
        [
            fine_unit(
                u, (left_ref, right_ref), ga_ref, proj_ref, wo_ref, gb_ref, wi_ref, wb_ref, mg_ref, mw_ref,
                (out_left, out_right), coarse_left, coarse_right, nat_ref.at[u], win_ref.at[u], table_ref, mixed_ref.at[u],
            )
            for u in range(units)
        ],
        LEAD if units > 1 else 0,
    )


def fine_unit(
    u, halves, ga_ref, proj_ref, wo_ref, gb_ref, wi_ref, wb_ref, mg_ref, mw_ref,
    outs, coarse_left, coarse_right, nat_ref, win_ref, table_ref, mixed_ref,
):
    width = wo_ref.shape[0]
    pair = 2 * width
    for l in range(2):
        for s in range(2):
            for p in range(3):
                at = l * 288 + (s * 3 + p) * 24
                x = halves[s][2 * u + l, :, p * pair : (p + 1) * pair].astype(F32)
                put_rows(nat_ref, at, x[:, :256])
                put_rows(nat_ref, at + 144, pltpu.roll(x[:, 128:], 192, axis=1))
    for src, dst in fine_moves():
        for t in range(2):
            win_ref[t, pl.ds(dst, 6, stride=2), :] = nat_ref[t, pl.ds(src, 6, stride=24), :]
    v = get_rows(win_ref, 0, 576)[:, :width]
    yield
    result = []
    yield from window_block(
        result, v, row(ga_ref), proj_ref[0], proj_ref[1], proj_ref[2], wo_ref[...],
        table_ref, row(gb_ref), wi_ref[...], wb_ref[...], mixed_ref,
    )
    done = result[0].astype(F32)
    put_rows(win_ref, 0, tiled(done))
    for src, dst in fine_moves():
        for t in range(2):
            nat_ref[t, pl.ds(src, 6, stride=24), :] = win_ref[t, pl.ds(dst, 6, stride=2), :]
    yield
    quarter = []
    for r in range(2):
        for c in range(2):
            quarter.append(
                jnp.concatenate(
                    [get_every_other(nat_ref, l * 288 + c * 144 + r, 72)[:, :width] for l in range(2)], axis=0
                )
            )
    mean = sum(jnp.sum(x, axis=-1, keepdims=True) for x in quarter) * (1.0 / (4 * width))
    center = [x - mean for x in quarter]
    spread = sum(jnp.sum(x * x, axis=-1, keepdims=True) for x in center) * (1.0 / (4 * width))
    scale = lax.rsqrt(spread + 1e-05)
    gains = row(mg_ref)
    coarse = 0.0
    for i in range(4):
        n = (center[i] * scale * gains[:, i * width : (i + 1) * width]).astype(BF)
        coarse = coarse + mm(n, mw_ref[i * width : (i + 1) * width])
    for l in range(2):
        coarse_left[u, l] = coarse[l * 72 : l * 72 + 36].astype(BF)
        coarse_right[u, l] = coarse[l * 72 + 36 : l * 72 + 72].astype(BF)
    yield
    low = lax.broadcasted_iota(jnp.int32, (24, 128), 1) < 64
    for l in range(2):
        for s in range(2):
            for p in range(3):
                at = l * 288 + (s * 3 + p) * 24
                even = get_rows(nat_ref, at, 24)
                odd = pltpu.roll(get_rows(nat_ref, at + 144, 24), 64, axis=1)
                middle = jnp.where(low, even[:, 128:], odd[:, :128])
                outs[s][2 * u + l, :, p * pair : (p + 1) * pair] = jnp.concatenate(
                    [even[:, :128], middle, odd[:, 128:]], axis=1
                ).astype(BF)


def coarse_kernel(
    g0, g1, g2, g3, cot_ref, cot_near_ref, cot_far_ref, bias_ref, ga_ref, wqkv_ref, wo_ref, gb_ref,
    wi_ref, wb_ref,
    done_own, done_next, packed_ref, nat_ref, win_ref, table_ref, mixed_ref, grad_ref,
):
    heads = bias_ref.shape[0]

    @pl.when(pl.program_id(0) == 0)
    def _():
        scaled_bias(bias_ref, table_ref, heads)
        grad_ref[...] = jnp.zeros_like(grad_ref)

    units = g0.shape[0]
    interleave(
        [
            coarse_unit(
                u, (g0, g1, g2, g3), cot_ref, cot_near_ref, cot_far_ref, ga_ref, wqkv_ref, wo_ref, gb_ref, wi_ref, wb_ref,
                done_own, done_next, grad_ref, nat_ref.at[u], win_ref.at[u], table_ref, mixed_ref.at[u],
            )
            for u in range(units)
        ],
        LEAD if units > 1 else 0,
    )

    @pl.when(pl.program_id(0) == pl.num_programs(0) - 1)
    def _():
        for j in range(128):
            t, b = divmod(j, 24)
            packed_ref[j, :16, :] = grad_ref[b * 16 : b * 16 + 16, t * 128 : (t + 1) * 128].astype(BF)
            packed_ref[j, 16:, :] = grad_ref[128 + 2 * j : 130 + 2 * j, 640:].astype(BF)


def sum_kernel(in_ref, out_ref):
    total = in_ref[0].astype(F32)
    for j in range(1, 128):
        total = total + in_ref[j].astype(F32)
    total = total.astype(BF)
    for j in range(128):
        out_ref[j] = total


def unpack_kernel(in_ref, out_ref):
    for j in range(128):
        t, b = divmod(j, 24)
        out_ref[b * 16 : b * 16 + 16, t * 128 : (t + 1) * 128] = in_ref[j, :16, :].astype(F32)
        out_ref[128 + 2 * j : 130 + 2 * j, 640:] = in_ref[j, 16:, :].astype(F32)


def coarse_unit(
    u, groups, cot_ref, cot_near_ref, cot_far_ref, ga_ref, wqkv_ref, wo_ref, gb_ref, wi_ref, wb_ref,
    done_own, done_next, grad_ref, nat_ref, win_ref, table_ref, mixed_ref,
):
    width = wo_ref.shape[0]
    for l in range(2):
        for i, g in enumerate(groups):
            put_rows(nat_ref, l * 144 + i * 36, g[u, l].astype(F32))
    moves = [(l * 144 + row, (row // 6) * 144 + l * 72 + (row % 6) * 12) for l in range(2) for row in range(12)]
    for src, dst in moves:
        for t in range(3):
            win_ref[t, dst : dst + 12, :] = nat_ref[t, pl.ds(src, 12, stride=12), :]
    yield
    result = []
    yield from window_block(
        result, get_rows(win_ref, 0, 288), row(ga_ref), wqkv_ref[:, :width], wqkv_ref[:, width : 2 * width],
        wqkv_ref[:, 2 * width :], wo_ref[...],
        table_ref, row(gb_ref), wi_ref[...], wb_ref[...], mixed_ref,
    )
    done = result[0]
    put_rows(win_ref, 0, done.astype(F32))
    for src, dst in moves:
        for t in range(3):
            nat_ref[t, pl.ds(src, 12, stride=12), :] = win_ref[t, dst : dst + 12, :]
    yield
    for half, out in enumerate((done_own, done_next)):
        tokens = jnp.concatenate([get_rows(nat_ref, l * 144 + half * 72, 72) for l in range(2)], axis=0).astype(BF)
        out[u] = tokens
        for l in range(2):
            for c in range(6):
                ref, at = (cot_ref, c) if half == 0 else (cot_near_ref, c) if c < 2 else (cot_far_ref, c - 2)
                put_rows(win_ref, (l * 6 + c) * 24, ref[2 * u + l, :, at * width : (at + 1) * width].astype(F32))
        for r in range(2):
            x = get_every_other(win_ref, r, 144).astype(BF)
            grad_ref[:, r * width : (r + 1) * width] += mm(tokens, x, TN)
        yield


def final_kernel(done_west, done_east, set0, set1, set2, set3, up_ref, out_ref, rows_ref):
    width = done_west.shape[2]
    halves = (set0, set1, set2, set3)
    for e, done_ref in enumerate((done_west, done_east)):
        raised = mm(done_ref[0], up_ref[...])
        for r in range(2):
            put_every_other(rows_ref, r, raised[:, r * width : (r + 1) * width])
        for l in range(2):
            for c in range(6):
                base = halves[2 * e + c // 3][l, :, (c % 3) * width : (c % 3 + 1) * width]
                total = base.astype(F32) + get_rows(rows_ref, (l * 6 + c) * 24, 24)
                out_ref[l, :, (e * 6 + c) * width : (e * 6 + c + 1) * width] = total.astype(BF)


def whole(a):
    return pl.BlockSpec(a.shape, lambda i: (0,) * a.ndim)


def params(mib):
    return pltpu.CompilerParams(vmem_limit_bytes=mib * MIB, dimension_semantics=("arbitrary",))


def fine_call(left, left_at, right, right_at, consts):
    levels, rows, _ = left.shape
    half = 1152
    steps = levels // (2 * UNITS)

    def spec(at):
        return pl.BlockSpec((2 * UNITS, rows, half), lambda i: (i, 0, at))

    cspec = pl.BlockSpec((UNITS, 2, 36, 384), lambda i: (i, 0, 0, 0))
    return pl.pallas_call(
        fine_kernel,
        grid=(steps,),
        in_specs=[spec(left_at), spec(right_at)] + [whole(c) for c in consts],
        out_specs=[spec(0), spec(0), cspec, cspec],
        out_shape=[jax.ShapeDtypeStruct((levels, rows, half), BF)] * 2
        + [jax.ShapeDtypeStruct((steps * UNITS, 2, 36, 384), BF)] * 2,
        scratch_shapes=[
            pltpu.VMEM((UNITS, 2, 640, 128), F32),
            pltpu.VMEM((UNITS, 2, 640, 128), F32),
            pltpu.VMEM((2, 24 * 144, 128), F32),
            pltpu.VMEM((UNITS, 576, 256), BF),
            pltpu.VMEM((3, 192, 256), BF),
        ],
        compiler_params=params(56),
        cost_estimate=pl.CostEstimate(flops=3 * 10**9, bytes_accessed=6 * 10**6, transcendentals=10**6),
    )(left, right, *consts)


def coarse_call(groups, cot, cot_near, cot_far, consts):
    steps = groups[0].shape[0] // UNITS
    gspec = pl.BlockSpec((UNITS, 2, 36, 384), lambda i: (i, 0, 0, 0))
    dspec = pl.BlockSpec((UNITS, 144, 384), lambda i: (i, 0, 0))
    return pl.pallas_call(
        coarse_kernel,
        grid=(steps,),
        in_specs=[gspec] * 4
        + [pl.BlockSpec((2 * UNITS, 24, 2304), lambda i: (i, 0, 1)), pl.BlockSpec((2 * UNITS, 24, 768), lambda i: (i, 0, 0)),
            pl.BlockSpec((2 * UNITS, 24, 1536), lambda i: (i, 0, 0))]
        + [whole(c) for c in consts],
        out_specs=[dspec, dspec, pl.BlockSpec((128, 18, 128), lambda i: (0, 0, 0))],
        out_shape=[jax.ShapeDtypeStruct((steps * UNITS, 144, 384), BF)] * 2
        + [jax.ShapeDtypeStruct((128, 18, 128), BF)],
        scratch_shapes=[
            pltpu.VMEM((UNITS, 3, 352, 128), F32),
            pltpu.VMEM((UNITS, 3, 352, 128), F32),
            pltpu.VMEM((2, 24 * 144, 128), F32),
            pltpu.VMEM((UNITS, 288, 384), BF),
            pltpu.VMEM((384, 768), F32),
        ],
        compiler_params=params(56),
        cost_estimate=pl.CostEstimate(flops=5 * 10**9, bytes_accessed=8 * 10**6, transcendentals=10**6),
    )(*groups, cot, cot_near, cot_far, *consts)


def final_call(done_west, done_east, quarters, up):
    steps = done_west.shape[0]
    dspec = pl.BlockSpec((1, 144, 384), lambda i: (i, 0, 0))
    sspec = pl.BlockSpec((2, 24, 1152), lambda i: (i, 0, 0))
    return pl.pallas_call(
        final_kernel,
        grid=(steps,),
        in_specs=[dspec] * 2 + [sspec] * 4 + [whole(up)],
        out_specs=pl.BlockSpec((2, 24, 4608), lambda i: (i, 0, 0)),
        out_shape=jax.ShapeDtypeStruct((2 * steps, 24, 4608), BF),
        scratch_shapes=[pltpu.VMEM((3, 288, 128), F32)],
        compiler_params=params(32),
        cost_estimate=pl.CostEstimate(flops=10**11, bytes_accessed=6 * 10**6, transcendentals=0),
    )(done_west, done_east, *quarters, up)


def passed_along(block, axis, distance):
    n = lax.axis_size(axis)
    return lax.ppermute(block, axis, [((i - distance) % n, i) for i in range(n)])


def packed_call(kernel, packed, shape, dtype):
    return pl.pallas_call(
        kernel,
        out_shape=jax.ShapeDtypeStruct(shape, dtype),
        in_specs=[pl.BlockSpec(memory_space=pltpu.VMEM)],
        out_specs=pl.BlockSpec(memory_space=pltpu.VMEM),
        compiler_params=pltpu.CompilerParams(vmem_limit_bytes=16 * MIB),
    )(packed)


def reduce_everywhere(packed, meanwhile):
    axes = ("lon", "lat")
    if lax.axis_size("lon") * lax.axis_size("lat") != packed.shape[0]:
        packed = lax.psum(packed.astype(F32), axes).astype(BF)
    else:
        parts = lax.all_to_all(packed, axes, 0, 0)
        parts, meanwhile = lax.optimization_barrier((parts, meanwhile))
        packed = lax.all_to_all(packed_call(sum_kernel, parts, packed.shape, BF), axes, 0, 0)
    return packed_call(unpack_kernel, packed, (384, 768), F32), meanwhile


def shards(
    field, cotangent,
    fine_gain_a, fine_qkv, fine_out, fine_bias, fine_gain_b, fine_in, fine_back,
    merge_gain, merge_weight,
    coarse_gain_a, coarse_qkv, coarse_out, coarse_bias, coarse_gain_b, coarse_in, coarse_back,
    up_weight,
):
    width = fine_qkv.shape[0]
    half = 6 * width
    near = 4 * width
    halo = passed_along(field[:, :, :half], "lon", -1)
    cot_near = passed_along(cotangent[:, :, :near], "lon", -1)
    fine_consts = (
        fine_bias,
        fine_gain_a, fine_qkv, fine_out, fine_gain_b, fine_in, fine_back, merge_gain, merge_weight,
    )
    coarse_consts = (
        coarse_bias,
        coarse_gain_a, coarse_qkv, coarse_out, coarse_gain_b, coarse_in, coarse_back,
    )
    a_left, a_right, ca_left, ca_right = fine_call(field, 1, field, 2, fine_consts)
    halo, cot_near, ca_left, a_left = lax.optimization_barrier((halo, cot_near, ca_left, a_left))
    ca_next = passed_along(ca_left, "lon", -1)
    cot_rest, a_left = lax.optimization_barrier((cotangent[:, :, near : 2 * half], a_left))
    cot_far = passed_along(cot_rest, "lon", -1)
    b_left, b_right, cb_left, cb_right = fine_call(field, 3, halo, 0, fine_consts)
    b_prev = passed_along(b_right, "lon", 1)
    done_own, done_next, packed = coarse_call((ca_right, cb_left, cb_right, ca_next), cotangent, cot_near, cot_far, coarse_consts)
    done_prev = passed_along(done_next, "lon", 1)
    packed, b_prev = lax.optimization_barrier((packed, b_prev))
    output = final_call(done_prev, done_own, (b_prev, a_left, a_right, b_left), up_weight)
    up_grad, output = reduce_everywhere(packed, output)
    return output, up_grad


def solution(mesh):
    lat = P(None, "lat", None)
    split = P(None, "lat", "lon")
    return jax.shard_map(
        shards,
        mesh=mesh,
        in_specs=(split, split, P(), P(), P(), lat) + (P(),) * 8 + (lat,) + (P(),) * 4,
        out_specs=(split, P()),
        check_vma=False,
    )
```
